128 devices in a mesh: lon: 16 (over y, z), day: 8 (over x, core).
Axes of the slice: x: 4, y: 4, z: 4, core: 2. Of those that a mesh axis runs over, the one named last changes fastest.
Arguments:
- latent: float32 [32, 1024, 2048], P('day', None, 'lon'), may hold values from -4 to 4
- range_sq: float32 [32, 1024, 2048], P('day', None, 'lon'), may hold values from 0.5 to 12
- counts: int32 [32, 1024, 2048], P('day', None, 'lon'), may hold values from 0 to 7
- land: int32 [32, 1024, 2048], P('day', None, 'lon'), may hold values 0 or 1
Outputs:
- step: float32 [32, 1024, 2048], P('day', None, 'lon')
- residual: float32 [32, 1024, 2048], P('day', None, 'lon')
The draws below stay inside these ranges and needn't reach their ends.
All inputs are finite; a program needn't handle non-finite values. No bound on the sum of `land` on one device may be relied on, other than what follows from the above.
Results may differ from the reference program's by a relative error of at most 0.00023.
Values sent between devices are 32-bit elements; how exact they have to be, the bound alone decides.
A program may use at most 64 MiB of HBM per device.

```python
import jax
import jax.numpy as jnp

LAT = 1024
ITERS = 2
LON = 2048
DAYS = 32


def draw_range_sq(key, part):
    shape = (DAYS, LAT, LON)
    trend = 1.0 + 2.0 * jnp.arange(LON, dtype=jnp.float32).reshape(1, 1, LON) / (LON - 1)
    logs = jax.random.uniform(key, shape, jnp.float32, jnp.log(0.5), jnp.log(4.0))
    base = jnp.exp(logs)
    return (base * trend).astype(jnp.float32)


def with_ends(values, own_key, low, high):
    index_at = [jax.random.randint(jax.random.fold_in(own_key, axis), (), 0, length) for axis, length in enumerate(values.shape)]
    main_axis = values.shape.index(max(values.shape))
    neighbour = index_at[:main_axis] + [(index_at[main_axis] + 1) % values.shape[main_axis]] + index_at[main_axis + 1:]
    return values.at[tuple(index_at)].set(low).at[tuple(neighbour)].set(high)


def level_of(key, shape, shards, smallest, high):
    factor_of, own = 1.0, jax.random.fold_in(key, 6)
    for axis_at, shards_of in shards:
        draws = jnp.exp(jax.random.uniform(jax.random.fold_in(own, axis_at), (shards_of,), jnp.float32, smallest / len(shards), high / len(shards)))
        factor_of = factor_of * jnp.repeat(draws, shape[axis_at] // shards_of).reshape([-1 if axis == axis_at else 1 for axis in range(len(shape))])
    return factor_of


def normal_values(stream_key, extent, deviation, bound, shards=(), held_as=jnp.bfloat16):
    result = jax.random.normal(stream_key, extent, jnp.float32) * deviation
    if len(shards) > 0:
        result = level_of(stream_key, extent, shards, -0.22, 0.18) * result
    return jnp.clip(result, min=-bound, max=bound).astype(held_as)


def setup_inputs(seed: int = 0) -> dict:
    seeds = jax.random.split(jax.random.key(seed), 5)
    return {
        "latent": normal_values(seeds[0], (DAYS, LAT, LON), 1.0, 4.0, ((0, 8), (2, 16)), jnp.float32),
        "range_sq": draw_range_sq(jax.random.fold_in(seeds[4], 71), 0),
        "counts": with_ends(jax.random.randint(seeds[2], (DAYS, LAT, LON), 0, 8), jax.random.fold_in(seeds[2], 1), 0, 7).astype(jnp.int32),
        "land": with_ends((jax.random.randint(seeds[3], (DAYS, LAT, LON), 0, 3) < 1).astype(jnp.int32), jax.random.fold_in(seeds[3], 1), 0, 1),
    }


prior_scale = 0.02


def apply_k(field, range_sq):
    lat_pad = jnp.pad(field, ((0, 0), (1, 1), (0, 0)))
    beside = jnp.roll(field, -1, 0) + jnp.roll(field, 1, 0)
    beside = beside + jnp.roll(field, -1, 2) + jnp.roll(field, 1, 2)
    beside = beside + lat_pad[:, 2:] + lat_pad[:, :-2]
    return (range_sq + 6.0) * field - beside


def apply_q(field, range_sq):
    return prior_scale * apply_k(apply_k(field, range_sq), range_sq)


def reference(latent, range_sq, counts, land):
    mask = land.astype(jnp.float32)
    weight = mask * jnp.exp(latent)
    rows = jnp.arange(LAT).reshape(1, LAT, 1)
    neighbours = 6.0 - (rows == 0).astype(jnp.float32) - (rows == LAT - 1).astype(jnp.float32)
    precond = prior_scale * ((range_sq + 6.0) ** 2 + neighbours) + weight
    residual = -(apply_q(latent, range_sq) + weight - mask * counts.astype(jnp.float32))
    step = jnp.zeros_like(latent)
    scaled = residual / precond
    direction = scaled
    rz_now = jnp.sum(residual * scaled)
    for turn in range(ITERS):
        image = apply_q(direction, range_sq) + weight * direction
        alpha = rz_now / jnp.sum(direction * image)
        step = step + alpha * direction
        residual = residual - alpha * image
        if turn + 1 < ITERS:
            scaled = residual / precond
            rz_next = jnp.sum(residual * scaled)
            direction = scaled + (rz_next / rz_now) * direction
            rz_now = rz_next
    return step, residual
```

```python
import functools

import jax
import jax.numpy as jnp
from jax import lax
from jax.experimental import pallas as pl
from jax.experimental.pallas import tpu as pltpu
from jax.sharding import PartitionSpec as P

ROUNDS = 3
SCALE = 0.02
PAD = 8
GROUP = 8
CHUNK = 128
BLOCK = 32
MESH = pl.DeviceIdType.MESH


def kernel(
    names, n_day, n_lon,
    lat_h, rs_h, cnt_h, land_h, step_h, res_h,
    latp, rs6, cnt, land, weight, inv, p0p, up, r0, q0, sres, kv0, kv1, kv2,
    psend, vrecv, precv, csend, crecv, redsend, redrecv,
    plane_ss, plane_rs, col_ss, col_rs, red_ss, red_rs, in_sem, out_sem,
):
    days, lats, lons = rs6.shape
    last = days - 1
    chunks = lats // CHUNK
    groups = CHUNK // GROUP
    blocks = CHUNK // BLOCK
    per_block = BLOCK // GROUP
    me_d = lax.axis_index("day")
    me_l = lax.axis_index("lon")

    def device(day, lon):
        where = {"day": day, "lon": lon}
        return tuple(where[n] for n in names)

    day_peer = [device(lax.rem(me_d + k, n_day), me_l) for k in range(n_day)]
    lon_peer = [device(me_d, lax.rem(me_l + k, n_lon)) for k in range(n_lon)]
    sides = (day_peer[n_day - 1], day_peer[1])
    beside = (lon_peer[n_lon - 1], lon_peer[1])

    body = pl.ds(PAD, lats)
    loads = [
        pltpu.make_async_copy(lat_h, latp.at[:, body], in_sem.at[0]),
        pltpu.make_async_copy(rs_h, rs6, in_sem.at[1]),
        pltpu.make_async_copy(land_h, land, in_sem.at[2]),
        pltpu.make_async_copy(cnt_h, cnt, in_sem.at[3]),
    ]
    for copy in loads:
        copy.start()

    barrier = pltpu.get_barrier_semaphore()
    for peer in day_peer[1:] + lon_peer[1:]:
        pl.semaphore_signal(barrier, inc=1, device_id=peer, device_id_type=MESH)
    pl.semaphore_wait(barrier, n_day + n_lon - 2)

    fields = (latp, p0p, up)
    kvs = (kv0, kv1, kv2)
    edges = (0, last)

    def plane(rnd, kind, c, side):
        rows = pl.ds(c * CHUNK, CHUNK)
        if kind == 0:
            if rnd == 0:
                src = lat_h.at[edges[side], rows]
            else:
                src = fields[rnd].at[edges[side], pl.ds(PAD + c * CHUNK, CHUNK)]
            dst = vrecv.at[rnd, 1 - side, rows]
        else:
            src = psend.at[rnd, side, rows]
            dst = precv.at[rnd, 1 - side, rows]
        return pltpu.make_async_remote_copy(
            src_ref=src, dst_ref=dst,
            send_sem=plane_ss.at[rnd, kind, c, side], recv_sem=plane_rs.at[rnd, kind, c, 1 - side],
            device_id=sides[side], device_id_type=MESH,
        )

    def column(rnd, kind, c, side):
        return pltpu.make_async_remote_copy(
            src_ref=csend.at[rnd, kind, c], dst_ref=crecv.at[rnd, kind, c, 1 - side],
            send_sem=col_ss.at[rnd, kind, c, side], recv_sem=col_rs.at[rnd, kind, c, 1 - side],
            device_id=beside[side], device_id_type=MESH,
        )

    def start_both(copy, rnd, kind, c):
        copy(rnd, kind, c, 0).start()
        copy(rnd, kind, c, 1).start()

    def wait_both(copy, rnd, kind, c):
        copy(rnd, kind, c, 0).wait_recv()
        copy(rnd, kind, c, 1).wait_recv()

    def first_planes(c, carry):
        start_both(plane, 0, 0, c)
        return carry

    lax.fori_loop(0, chunks, first_planes, 0)

    lane = lax.broadcasted_iota(jnp.int32, (GROUP, lons), 1)
    pair = ((lane + 1) & (lons - 1)) >> 1
    lane_block = lax.broadcasted_iota(jnp.int32, (BLOCK, lons), 1)
    at_low = lane_block == 0
    at_high = lane_block == lons - 1
    even = (lane & 1) == 0
    zeros = jnp.zeros((GROUP, lons), jnp.float32)

    def gather(acc, tile, d, b):
        for k in range(per_block):
            j = d * groups + b * per_block + k
            acc = jnp.where(pair == j, pltpu.roll(tile[k * GROUP:(k + 1) * GROUP], 2 * j, 1), acc)
        return acc

    def outer_columns(rnd, kind, c):
        low = crecv[rnd, kind, c, 0]
        high = crecv[rnd, kind, c, 1]
        return jnp.where(even, pltpu.roll(low, 1, 1), pltpu.roll(high, lons - 1, 1))

    def along_lon(x, cols, d, b):
        outer = jnp.concatenate(
            [pltpu.roll(cols, (0 - 2 * (d * groups + b * per_block + k)) & (lons - 1), 1) for k in range(per_block)], axis=0
        )
        return jnp.where(at_low, outer, pltpu.roll(x, 1, 1)) + jnp.where(at_high, outer, pltpu.roll(x, lons - 1, 1))

    def own_part(ref, cols, row, b):
        x = [ref[d, pl.ds(PAD + row, BLOCK)] for d in range(days)]
        out = []
        for d in range(days):
            near = ref[d, pl.ds(PAD - 1 + row, BLOCK)] + ref[d, pl.ds(PAD + 1 + row, BLOCK)]
            near = near + along_lon(x[d], cols, d, b)
            if d > 0:
                near = near + x[d - 1]
            if d < last:
                near = near + x[d + 1]
            out.append(rs6[d, pl.ds(row, BLOCK)] * x[d] - near)
        return out

    def send_columns(rnd, kind, c, acc):
        csend[rnd, kind, c] = acc
        start_both(column, rnd, kind, c)

    def first_k(rnd, c, total):
        wait_both(column, rnd, 0, c)
        cols = outer_columns(rnd, 0, c)
        field, kv = fields[rnd], kvs[rnd]

        def partial(b, carry):
            row = pl.multiple_of(c * CHUNK + b * BLOCK, BLOCK)
            out = own_part(field, cols, row, b)
            rows = pl.ds(row, BLOCK)
            psend[rnd, 0, rows] = out[0]
            psend[rnd, 1, rows] = out[last]
            for d in range(1, last):
                kv[d, pl.ds(PAD + row, BLOCK)] = out[d]
            return carry

        lax.fori_loop(0, blocks, partial, 0)
        start_both(plane, rnd, 1, c)
        wait_both(plane, rnd, 0, c)

        def complete(b, carry):
            acc, total = carry
            row = pl.multiple_of(c * CHUNK + b * BLOCK, BLOCK)
            rows = pl.ds(row, BLOCK)
            for d in range(days):
                if d == 0 or d == last:
                    side = 0 if d == 0 else 1
                    tile = psend[rnd, side, rows] - vrecv[rnd, side, rows]
                    kv[d, pl.ds(PAD + row, BLOCK)] = tile
                else:
                    tile = kv[d, pl.ds(PAD + row, BLOCK)]
                acc = gather(acc, tile, d, b)
                if rnd == 1:
                    p = field[d, pl.ds(PAD + row, BLOCK)]
                    total = total + fold(SCALE * tile * tile + weight[d, rows] * p * p)
            return acc, total

        acc, total = lax.fori_loop(0, blocks, complete, (zeros, total))
        send_columns(rnd, 1, c, acc)
        return total

    def fold(x):
        return sum(x[k * GROUP:(k + 1) * GROUP] for k in range(1, per_block)) + x[:GROUP]

    def second_k(rnd, c, total):
        wait_both(column, rnd, 1, c)
        wait_both(plane, rnd, 1, c)
        cols = outer_columns(rnd, 1, c)
        field, kv = fields[rnd], kvs[rnd]

        def rest(b, carry):
            acc, total = carry
            row = pl.multiple_of(c * CHUNK + b * BLOCK, BLOCK)
            rows = pl.ds(row, BLOCK)
            wide = pl.ds(PAD + row, BLOCK)
            out = own_part(kv, cols, row, b)
            out[0] = out[0] - (precv[rnd, 0, rows] - field[0, wide])
            out[last] = out[last] - (precv[rnd, 1, rows] - field[last, wide])
            for d in range(days):
                image = SCALE * out[d]
                if rnd == 0:
                    base = sres[d, rows]
                    residual = 0.0 - (image + base)
                    value = residual * inv[d, rows]
                    r0[d, rows] = residual
                    p0p[d, wide] = value
                    total = total + fold(residual * value)
                else:
                    image = image + weight[d, rows] * field[d, wide]
                    if rnd == 1:
                        value = image * inv[d, rows]
                        q0[d, rows] = image
                        up[d, wide] = value
                    else:
                        sres[d, rows] = image
                if rnd < ROUNDS - 1:
                    acc = gather(acc, value, d, b)
            return acc, total

        acc, total = lax.fori_loop(0, blocks, rest, (zeros, total))
        if rnd < ROUNDS - 1:
            start_both(plane, rnd + 1, 0, c)
            send_columns(rnd + 1, 0, c, acc)
        return total

    count = redsend.shape[2]

    def peer_copy(which, stage, k):
        peers = (lon_peer, day_peer)[stage]
        return pltpu.make_async_remote_copy(
            src_ref=redsend.at[which, stage], dst_ref=redrecv.at[which, stage, k],
            send_sem=red_ss.at[which, stage, k], recv_sem=red_rs.at[which, stage, k],
            device_id=peers[k], device_id_type=MESH,
        )

    def reduce_start(which, stage, values):
        for i, v in enumerate(values):
            redsend[which, stage, i] = v
        for k in range(1, (n_lon, n_day)[stage]):
            peer_copy(which, stage, k).start()

    def reduce_wait(which, stage, used):
        n = (n_lon, n_day)[stage]
        for k in range(1, n):
            peer_copy(which, stage, k).wait_recv()
        out = []
        for i in range(used):
            total = redsend[which, stage, i]
            for k in range(1, n):
                total = total + redrecv[which, stage, k, i]
            out.append(total)
        return out

    def scalar(x):
        return jnp.sum(x)

    loads[0].wait()
    for ref in (latp, p0p, up, kv0, kv1, kv2):
        for d in range(days):
            ref[d, pl.ds(0, PAD)] = zeros
            ref[d, pl.ds(PAD + lats, PAD)] = zeros

    def first_columns(c, carry):
        def step(b, acc):
            row = pl.multiple_of(c * CHUNK + b * BLOCK, BLOCK)
            for d in range(days):
                acc = gather(acc, latp[d, pl.ds(PAD + row, BLOCK)], d, b)
            return acc

        send_columns(0, 0, c, lax.fori_loop(0, blocks, step, zeros))
        return carry

    lax.fori_loop(0, chunks, first_columns, 0)

    for copy in loads[1:]:
        copy.wait()

    def prepare(b, carry):
        row = pl.multiple_of(b * BLOCK, BLOCK)
        rows = pl.ds(row, BLOCK)
        at = row + lax.broadcasted_iota(jnp.int32, (BLOCK, lons), 0)
        near = 6.0 - jnp.where(at == 0, 1.0, 0.0) - jnp.where(at == lats - 1, 1.0, 0.0)
        for d in range(days):
            mask = land[d, rows].astype(jnp.float32)
            w = mask * jnp.exp(latp[d, pl.ds(PAD + row, BLOCK)])
            diag = rs6[d, rows] + 6.0
            rs6[d, rows] = diag
            weight[d, rows] = w
            inv[d, rows] = 1.0 / (SCALE * (diag * diag + near) + w)
            sres[d, rows] = w - mask * cnt[d, rows].astype(jnp.float32)
        return carry

    lax.fori_loop(0, lats // BLOCK, prepare, 0)

    m0 = m1 = zeros
    for rnd in range(ROUNDS):
        m1 = lax.fori_loop(0, chunks, functools.partial(first_k, rnd), m1)
        if rnd == 1:
            reduce_start(0, 0, [m0, m1])
        if rnd == 2:
            s0, s1 = [scalar(v) for v in reduce_wait(0, 1, 2)]
            rz0 = s0
            a0 = jnp.full((BLOCK, lons), s0) / jnp.full((BLOCK, lons), s1)

            def sums(b, carry):
                rz, zq, zz = carry
                row = pl.multiple_of(b * BLOCK, BLOCK)
                rows = pl.ds(row, BLOCK)
                wide = pl.ds(PAD + row, BLOCK)
                for d in range(days):
                    q = q0[d, rows]
                    z = p0p[d, wide] - a0 * up[d, wide]
                    kz = kv1[d, wide] - a0 * kv2[d, wide]
                    rz = rz + fold((r0[d, rows] - a0 * q) * z)
                    zq = zq + fold(z * q)
                    zz = zz + fold(SCALE * kz * kz + weight[d, rows] * z * z)
                return rz, zq, zz

            reduce_start(1, 0, lax.fori_loop(0, lats // BLOCK, sums, (zeros, zeros, zeros)))
        turn = functools.partial(second_k, rnd)
        if rnd == 0:
            m0 = lax.fori_loop(0, chunks, turn, m0)
        else:
            split = chunks - 2
            lax.fori_loop(0, split, turn, zeros)
            reduce_start(rnd - 1, 1, reduce_wait(rnd - 1, 0, (2, 3)[rnd - 1]))
            lax.fori_loop(split, chunks, turn, zeros)

    t0, t1, t2 = [scalar(v) for v in reduce_wait(1, 1, 3)]
    wide_of = lambda v: jnp.full((BLOCK, lons), v)
    rz1, zq, zz = wide_of(t0), wide_of(t1), wide_of(t2)
    beta = rz1 / wide_of(rz0)
    a1 = rz1 / (zz + 2.0 * beta * zq + beta * beta * wide_of(s1))
    coef_p = a0 + a1 * (1.0 + beta)
    coef_u = a0 * a1

    def out_copies(c):
        rows = pl.ds(c * CHUNK, CHUNK)
        return (
            pltpu.make_async_copy(q0.at[:, rows], step_h.at[:, rows], out_sem.at[0, c]),
            pltpu.make_async_copy(sres.at[:, rows], res_h.at[:, rows], out_sem.at[1, c]),
        )

    def finish(c, carry):
        def one(b, carry):
            row = pl.multiple_of(c * CHUNK + b * BLOCK, BLOCK)
            rows = pl.ds(row, BLOCK)
            wide = pl.ds(PAD + row, BLOCK)
            for d in range(days):
                q = q0[d, rows]
                sres[d, rows] = r0[d, rows] - coef_p * q + coef_u * sres[d, rows]
                q0[d, rows] = coef_p * p0p[d, wide] - coef_u * up[d, wide]
            return carry

        lax.fori_loop(0, blocks, one, 0)
        for copy in out_copies(c):
            copy.start()
        return carry

    lax.fori_loop(0, chunks, finish, 0)

    def drain(c, carry):
        for copy in out_copies(c):
            copy.wait()
        for rnd in range(ROUNDS):
            for kind in range(2):
                for side in range(2):
                    plane(rnd, kind, c, side).wait_send()
                    column(rnd, kind, c, side).wait_send()
        return carry

    lax.fori_loop(0, chunks, drain, 0)
    for which in range(2):
        for stage in range(2):
            for k in range(1, (n_lon, n_day)[stage]):
                peer_copy(which, stage, k).wait_send()


def solution(mesh):
    names = tuple(mesh.axis_names)
    n_day, n_lon = mesh.shape["day"], mesh.shape["lon"]
    spec = P("day", None, "lon")

    def per_device(latent, range_sq, counts, land):
        days, lats, lons = latent.shape
        chunks = lats // CHUNK
        f32 = jnp.float32
        whole = (days, lats, lons)
        padded = (days, lats + 2 * PAD, lons)
        vmem = pltpu.VMEM
        dma = pltpu.SemaphoreType.DMA
        return pl.pallas_call(
            functools.partial(kernel, names, n_day, n_lon),
            out_shape=[jax.ShapeDtypeStruct(whole, f32)] * 2,
            in_specs=[pl.BlockSpec(memory_space=pl.ANY)] * 4,
            out_specs=[pl.BlockSpec(memory_space=pl.ANY)] * 2,
            scratch_shapes=[
                vmem(padded, f32), vmem(whole, f32), vmem(whole, jnp.int32), vmem(whole, jnp.int32),
                vmem(whole, f32), vmem(whole, f32), vmem(padded, f32), vmem(padded, f32),
                vmem(whole, f32), vmem(whole, f32), vmem(whole, f32),
                vmem(padded, f32), vmem(padded, f32), vmem(padded, f32),
                vmem((ROUNDS, 2, lats, lons), f32), vmem((ROUNDS, 2, lats, lons), f32),
                vmem((ROUNDS, 2, lats, lons), f32),
                vmem((ROUNDS, 2, chunks, GROUP, lons), f32), vmem((ROUNDS, 2, chunks, 2, GROUP, lons), f32),
                vmem((2, 2, 3, GROUP, lons), f32), vmem((2, 2, n_lon, 3, GROUP, lons), f32),
                dma((ROUNDS, 2, chunks, 2)), dma((ROUNDS, 2, chunks, 2)),
                dma((ROUNDS, 2, chunks, 2)), dma((ROUNDS, 2, chunks, 2)),
                dma((2, 2, n_lon)), dma((2, 2, n_lon)), dma((4,)), dma((2, chunks)),
            ],
            compiler_params=pltpu.CompilerParams(
                collective_id=0, has_side_effects=True, vmem_limit_bytes=60 << 20
            ),
        )(latent, range_sq, counts, land)

    return jax.shard_map(per_device, mesh=mesh, in_specs=(spec,) * 4, out_specs=(spec, spec), check_vma=False)
```

```python
import functools

import jax
import jax.numpy as jnp
from jax import lax
from jax.experimental import pallas as pl
from jax.experimental.pallas import tpu as pltpu
from jax.sharding import PartitionSpec as P

ROUNDS = 3
SCALE = 0.02
PAD = 8
GROUP = 8
CHUNK = 128
BLOCK = 128
SMALL = 32
MESH = pl.DeviceIdType.MESH


def kernel(
    names, n_day, n_lon,
    lat_h, rs_h, cnt_h, land_h, step_h, res_h,
    latp, rs6, cnt, land, weight, inv, p0p, up, r0, q0, sres, kv0, kv1, kv2,
    psend, vrecv, precv, csend, crecv, redsend, redrecv,
    plane_ss, plane_rs, col_ss, col_rs, red_ss, red_rs, in_sem, out_sem,
):
    days, lats, lons = rs6.shape
    last = days - 1
    chunks = lats // CHUNK
    groups = CHUNK // GROUP
    blocks = CHUNK // BLOCK
    per_block = BLOCK // GROUP
    me_d = lax.axis_index("day")
    me_l = lax.axis_index("lon")

    def device(day, lon):
        where = {"day": day, "lon": lon}
        return tuple(where[n] for n in names)

    day_peer = [device(lax.rem(me_d + k, n_day), me_l) for k in range(n_day)]
    lon_peer = [device(me_d, lax.rem(me_l + k, n_lon)) for k in range(n_lon)]
    sides = (day_peer[n_day - 1], day_peer[1])
    beside = (lon_peer[n_lon - 1], lon_peer[1])

    body = pl.ds(PAD, lats)
    loads = [
        pltpu.make_async_copy(lat_h, latp.at[:, body], in_sem.at[0]),
        pltpu.make_async_copy(rs_h, rs6, in_sem.at[1]),
        pltpu.make_async_copy(land_h, land, in_sem.at[2]),
        pltpu.make_async_copy(cnt_h, cnt, in_sem.at[3]),
    ]
    for copy in loads:
        copy.start()

    barrier = pltpu.get_barrier_semaphore()
    for peer in day_peer[1:] + lon_peer[1:]:
        pl.semaphore_signal(barrier, inc=1, device_id=peer, device_id_type=MESH)
    pl.semaphore_wait(barrier, n_day + n_lon - 2)

    fields = (latp, p0p, up)
    kvs = (kv0, kv1, kv2)
    edges = (0, last)

    def plane(rnd, kind, c, side):
        rows = pl.ds(c * CHUNK, CHUNK)
        if kind == 0:
            if rnd == 0:
                src = lat_h.at[edges[side], rows]
            else:
                src = fields[rnd].at[edges[side], pl.ds(PAD + c * CHUNK, CHUNK)]
            dst = vrecv.at[rnd, 1 - side, rows]
        else:
            src = psend.at[rnd, side, rows]
            dst = precv.at[rnd, 1 - side, rows]
        return pltpu.make_async_remote_copy(
            src_ref=src, dst_ref=dst,
            send_sem=plane_ss.at[rnd, kind, c, side], recv_sem=plane_rs.at[rnd, kind, c, 1 - side],
            device_id=sides[side], device_id_type=MESH,
        )

    def column(rnd, kind, c, side):
        return pltpu.make_async_remote_copy(
            src_ref=csend.at[rnd, kind, c], dst_ref=crecv.at[rnd, kind, c, 1 - side],
            send_sem=col_ss.at[rnd, kind, c, side], recv_sem=col_rs.at[rnd, kind, c, 1 - side],
            device_id=beside[side], device_id_type=MESH,
        )

    def unrolled(n, body, carry):
        for i in range(n):
            carry = body(i, carry)
        return carry

    def start_both(copy, rnd, kind, c):
        copy(rnd, kind, c, 0).start()
        copy(rnd, kind, c, 1).start()

    def wait_both(copy, rnd, kind, c):
        copy(rnd, kind, c, 0).wait_recv()
        copy(rnd, kind, c, 1).wait_recv()

    def first_planes(c, carry):
        start_both(plane, 0, 0, c)
        return carry

    lax.fori_loop(0, chunks, first_planes, 0)

    lane = lax.broadcasted_iota(jnp.int32, (GROUP, lons), 1)
    pair = ((lane + 1) & (lons - 1)) >> 1
    lane_block = lax.broadcasted_iota(jnp.int32, (BLOCK, lons), 1)
    at_low = lane_block == 0
    at_high = lane_block == lons - 1
    even = (lane & 1) == 0
    zeros = jnp.zeros((GROUP, lons), jnp.float32)

    def gather(tile, d, b):
        acc = zeros
        for k in range(per_block):
            j = d * groups + b * per_block + k
            acc = jnp.where(pair == j, pltpu.roll(tile[k * GROUP:(k + 1) * GROUP], (2 * j) % lons, 1), acc)
        return acc

    def outer_columns(rnd, kind, c):
        low = crecv[rnd, kind, c, 0]
        high = crecv[rnd, kind, c, 1]
        return jnp.where(even, pltpu.roll(low, 1, 1), pltpu.roll(high, lons - 1, 1))

    def along_lon(x, cols, d, b):
        outer = jnp.concatenate(
            [pltpu.roll(cols, (0 - 2 * (d * groups + b * per_block + k)) % lons, 1) for k in range(per_block)], axis=0
        )
        return jnp.where(at_low, outer, pltpu.roll(x, 1, 1)) + jnp.where(at_high, outer, pltpu.roll(x, lons - 1, 1))

    def own_part(ref, cols, row, b):
        x = [ref[d, pl.ds(PAD + row, BLOCK)] for d in range(days)]
        out = []
        for d in range(days):
            near = ref[d, pl.ds(PAD - 1 + row, BLOCK)] + ref[d, pl.ds(PAD + 1 + row, BLOCK)]
            near = near + along_lon(x[d], cols, d, b)
            if d > 0:
                near = near + x[d - 1]
            if d < last:
                near = near + x[d + 1]
            out.append(rs6[d, pl.ds(row, BLOCK)] * x[d] - near)
        return out

    def send_columns(rnd, kind, c, acc):
        csend[rnd, kind, c] = acc
        start_both(column, rnd, kind, c)

    def first_k(rnd, c, total):
        wait_both(column, rnd, 0, c)
        cols = outer_columns(rnd, 0, c)
        field, kv = fields[rnd], kvs[rnd]

        def partial(b, carry):
            row = pl.multiple_of(c * CHUNK + b * BLOCK, BLOCK)
            out = own_part(field, cols, row, b)
            rows = pl.ds(row, BLOCK)
            psend[rnd, 0, rows] = out[0]
            psend[rnd, 1, rows] = out[last]
            for d in range(1, last):
                kv[d, pl.ds(PAD + row, BLOCK)] = out[d]
            return carry

        unrolled(blocks, partial, 0)
        start_both(plane, rnd, 1, c)
        wait_both(plane, rnd, 0, c)

        def complete(b, carry):
            acc, total = carry
            row = pl.multiple_of(c * CHUNK + b * BLOCK, BLOCK)
            rows = pl.ds(row, BLOCK)
            for d in range(days):
                if d == 0 or d == last:
                    side = 0 if d == 0 else 1
                    tile = psend[rnd, side, rows] - vrecv[rnd, side, rows]
                    kv[d, pl.ds(PAD + row, BLOCK)] = tile
                else:
                    tile = kv[d, pl.ds(PAD + row, BLOCK)]
                acc = acc + gather(tile, d, b)
                if rnd == 1:
                    p = field[d, pl.ds(PAD + row, BLOCK)]
                    total = total + fold(SCALE * tile * tile + weight[d, rows] * p * p)
            return acc, total

        acc, total = unrolled(blocks, complete, (zeros, total))
        send_columns(rnd, 1, c, acc)
        return total

    def fold(x):
        while x.shape[0] > GROUP:
            half = x.shape[0] // 2
            x = x[:half] + x[half:]
        return x

    def second_k(rnd, c, total):
        wait_both(column, rnd, 1, c)
        wait_both(plane, rnd, 1, c)
        cols = outer_columns(rnd, 1, c)
        field, kv = fields[rnd], kvs[rnd]

        def rest(b, carry):
            acc, total = carry
            row = pl.multiple_of(c * CHUNK + b * BLOCK, BLOCK)
            rows = pl.ds(row, BLOCK)
            wide = pl.ds(PAD + row, BLOCK)
            out = own_part(kv, cols, row, b)
            out[0] = out[0] - (precv[rnd, 0, rows] - field[0, wide])
            out[last] = out[last] - (precv[rnd, 1, rows] - field[last, wide])
            for d in range(days):
                image = SCALE * out[d]
                if rnd == 0:
                    base = sres[d, rows]
                    residual = 0.0 - (image + base)
                    value = residual * inv[d, rows]
                    r0[d, rows] = residual
                    p0p[d, wide] = value
                    total = total + fold(residual * value)
                else:
                    image = image + weight[d, rows] * field[d, wide]
                    if rnd == 1:
                        value = image * inv[d, rows]
                        q0[d, rows] = image
                        up[d, wide] = value
                    else:
                        sres[d, rows] = image
                if rnd < ROUNDS - 1:
                    acc = acc + gather(value, d, b)
            return acc, total

        acc, total = unrolled(blocks, rest, (zeros, total))
        if rnd < ROUNDS - 1:
            start_both(plane, rnd + 1, 0, c)
            send_columns(rnd + 1, 0, c, acc)
        return total

    count = redsend.shape[2]

    def peer_copy(which, stage, k):
        peers = (lon_peer, day_peer)[stage]
        return pltpu.make_async_remote_copy(
            src_ref=redsend.at[which, stage], dst_ref=redrecv.at[which, stage, k],
            send_sem=red_ss.at[which, stage, k], recv_sem=red_rs.at[which, stage, k],
            device_id=peers[k], device_id_type=MESH,
        )

    def reduce_start(which, stage, values):
        for i, v in enumerate(values):
            redsend[which, stage, i] = v
        for k in range(1, (n_lon, n_day)[stage]):
            peer_copy(which, stage, k).start()

    def reduce_wait(which, stage, used):
        n = (n_lon, n_day)[stage]
        for k in range(1, n):
            peer_copy(which, stage, k).wait_recv()
        out = []
        for i in range(used):
            total = redsend[which, stage, i]
            for k in range(1, n):
                total = total + redrecv[which, stage, k, i]
            out.append(total)
        return out

    def scalar(x):
        return jnp.sum(x)

    loads[0].wait()
    for ref in (latp, p0p, up, kv0, kv1, kv2):
        for d in range(days):
            ref[d, pl.ds(0, PAD)] = zeros
            ref[d, pl.ds(PAD + lats, PAD)] = zeros

    def first_columns(c, carry):
        def step(b, acc):
            row = pl.multiple_of(c * CHUNK + b * BLOCK, BLOCK)
            for d in range(days):
                acc = acc + gather(latp[d, pl.ds(PAD + row, BLOCK)], d, b)
            return acc

        send_columns(0, 0, c, unrolled(blocks, step, zeros))
        return carry

    lax.fori_loop(0, chunks, first_columns, 0)

    for copy in loads[1:]:
        copy.wait()

    def prepare(b, carry):
        row = pl.multiple_of(b * SMALL, SMALL)
        rows = pl.ds(row, SMALL)
        at = row + lax.broadcasted_iota(jnp.int32, (SMALL, lons), 0)
        near = 6.0 - jnp.where(at == 0, 1.0, 0.0) - jnp.where(at == lats - 1, 1.0, 0.0)
        for d in range(days):
            mask = land[d, rows].astype(jnp.float32)
            w = mask * jnp.exp(latp[d, pl.ds(PAD + row, SMALL)])
            diag = rs6[d, rows] + 6.0
            rs6[d, rows] = diag
            weight[d, rows] = w
            inv[d, rows] = 1.0 / (SCALE * (diag * diag + near) + w)
            sres[d, rows] = w - mask * cnt[d, rows].astype(jnp.float32)
        return carry

    lax.fori_loop(0, lats // SMALL, prepare, 0)

    m0 = m1 = zeros
    for rnd in range(ROUNDS):
        m1 = lax.fori_loop(0, chunks, functools.partial(first_k, rnd), m1)
        if rnd == 1:
            reduce_start(0, 0, [m0, m1])
        if rnd == 2:
            s0, s1 = [scalar(v) for v in reduce_wait(0, 1, 2)]
            rz0 = s0
            a0 = jnp.full((SMALL, lons), s0) / jnp.full((SMALL, lons), s1)

            def sums(b, carry):
                rz, zq, zz = carry
                row = pl.multiple_of(b * SMALL, SMALL)
                rows = pl.ds(row, SMALL)
                wide = pl.ds(PAD + row, SMALL)
                for d in range(days):
                    q = q0[d, rows]
                    z = p0p[d, wide] - a0 * up[d, wide]
                    kz = kv1[d, wide] - a0 * kv2[d, wide]
                    rz = rz + fold((r0[d, rows] - a0 * q) * z)
                    zq = zq + fold(z * q)
                    zz = zz + fold(SCALE * kz * kz + weight[d, rows] * z * z)
                return rz, zq, zz

            reduce_start(1, 0, lax.fori_loop(0, lats // SMALL, sums, (zeros, zeros, zeros)))
        turn = functools.partial(second_k, rnd)
        if rnd == 0:
            m0 = lax.fori_loop(0, chunks, turn, m0)
        else:
            split = chunks - 2
            lax.fori_loop(0, split, turn, zeros)
            reduce_start(rnd - 1, 1, reduce_wait(rnd - 1, 0, (2, 3)[rnd - 1]))
            lax.fori_loop(split, chunks, turn, zeros)

    t0, t1, t2 = [scalar(v) for v in reduce_wait(1, 1, 3)]
    wide_of = lambda v: jnp.full((SMALL, lons), v)
    rz1, zq, zz = wide_of(t0), wide_of(t1), wide_of(t2)
    beta = rz1 / wide_of(rz0)
    a1 = rz1 / (zz + 2.0 * beta * zq + beta * beta * wide_of(s1))
    coef_p = a0 + a1 * (1.0 + beta)
    coef_u = a0 * a1

    def out_copies(c):
        rows = pl.ds(c * CHUNK, CHUNK)
        return (
            pltpu.make_async_copy(q0.at[:, rows], step_h.at[:, rows], out_sem.at[0, c]),
            pltpu.make_async_copy(sres.at[:, rows], res_h.at[:, rows], out_sem.at[1, c]),
        )

    def finish(c, carry):
        def one(b, carry):
            row = pl.multiple_of(c * CHUNK + b * SMALL, SMALL)
            rows = pl.ds(row, SMALL)
            wide = pl.ds(PAD + row, SMALL)
            for d in range(days):
                q = q0[d, rows]
                sres[d, rows] = r0[d, rows] - coef_p * q + coef_u * sres[d, rows]
                q0[d, rows] = coef_p * p0p[d, wide] - coef_u * up[d, wide]
            return carry

        lax.fori_loop(0, CHUNK // SMALL, one, 0)
        for copy in out_copies(c):
            copy.start()
        return carry

    lax.fori_loop(0, chunks, finish, 0)

    def drain(c, carry):
        for copy in out_copies(c):
            copy.wait()
        for rnd in range(ROUNDS):
            for kind in range(2):
                for side in range(2):
                    plane(rnd, kind, c, side).wait_send()
                    column(rnd, kind, c, side).wait_send()
        return carry

    lax.fori_loop(0, chunks, drain, 0)
    for which in range(2):
        for stage in range(2):
            for k in range(1, (n_lon, n_day)[stage]):
                peer_copy(which, stage, k).wait_send()


def solution(mesh):
    names = tuple(mesh.axis_names)
    n_day, n_lon = mesh.shape["day"], mesh.shape["lon"]
    spec = P("day", None, "lon")

    def per_device(latent, range_sq, counts, land):
        days, lats, lons = latent.shape
        chunks = lats // CHUNK
        f32 = jnp.float32
        whole = (days, lats, lons)
        padded = (days, lats + 2 * PAD, lons)
        vmem = pltpu.VMEM
        dma = pltpu.SemaphoreType.DMA
        return pl.pallas_call(
            functools.partial(kernel, names, n_day, n_lon),
            out_shape=[jax.ShapeDtypeStruct(whole, f32)] * 2,
            in_specs=[pl.BlockSpec(memory_space=pl.ANY)] * 4,
            out_specs=[pl.BlockSpec(memory_space=pl.ANY)] * 2,
            scratch_shapes=[
                vmem(padded, f32), vmem(whole, f32), vmem(whole, jnp.int32), vmem(whole, jnp.int32),
                vmem(whole, f32), vmem(whole, f32), vmem(padded, f32), vmem(padded, f32),
                vmem(whole, f32), vmem(whole, f32), vmem(whole, f32),
                vmem(padded, f32), vmem(padded, f32), vmem(padded, f32),
                vmem((ROUNDS, 2, lats, lons), f32), vmem((ROUNDS, 2, lats, lons), f32),
                vmem((ROUNDS, 2, lats, lons), f32),
                vmem((ROUNDS, 2, chunks, GROUP, lons), f32), vmem((ROUNDS, 2, chunks, 2, GROUP, lons), f32),
                vmem((2, 2, 3, GROUP, lons), f32), vmem((2, 2, n_lon, 3, GROUP, lons), f32),
                dma((ROUNDS, 2, chunks, 2)), dma((ROUNDS, 2, chunks, 2)),
                dma((ROUNDS, 2, chunks, 2)), dma((ROUNDS, 2, chunks, 2)),
                dma((2, 2, n_lon)), dma((2, 2, n_lon)), dma((4,)), dma((2, chunks)),
            ],
            compiler_params=pltpu.CompilerParams(
                collective_id=0, has_side_effects=True, vmem_limit_bytes=60 << 20
            ),
        )(latent, range_sq, counts, land)

    return jax.shard_map(per_device, mesh=mesh, in_specs=(spec,) * 4, out_specs=(spec, spec), check_vma=False)
```

```python
import functools

import jax
import jax.numpy as jnp
from jax import lax
from jax.experimental import pallas as pl
from jax.experimental.pallas import tpu as pltpu
from jax.sharding import PartitionSpec as P

ROUNDS = 3
SCALE = 0.02
PAD = 8
GROUP = 8
CHUNK = 128
BLOCK = 128
SMALL = 64
MESH = pl.DeviceIdType.MESH


def kernel(
    names, n_day, n_lon,
    lat_h, rs_h, cnt_h, land_h, p0p, up, r0, q0, sres, coefs,
    latp, rs6, cnt, land, weight, inv, kv0, kv1, kv2,
    psend, vrecv, precv, csend, crecv, redsend, redrecv,
    plane_ss, plane_rs, col_ss, col_rs, red_ss, red_rs, in_sem,
):
    days, lats, lons = rs6.shape
    last = days - 1
    chunks = lats // CHUNK
    groups = CHUNK // GROUP
    blocks = CHUNK // BLOCK
    per_block = BLOCK // GROUP
    me_d = lax.axis_index("day")
    me_l = lax.axis_index("lon")

    def device(day, lon):
        where = {"day": day, "lon": lon}
        return tuple(where[n] for n in names)

    day_peer = [device(lax.rem(me_d + k, n_day), me_l) for k in range(n_day)]
    lon_peer = [device(me_d, lax.rem(me_l + k, n_lon)) for k in range(n_lon)]
    sides = (day_peer[n_day - 1], day_peer[1])
    beside = (lon_peer[n_lon - 1], lon_peer[1])

    body = pl.ds(PAD, lats)
    loads = [
        pltpu.make_async_copy(lat_h, latp.at[:, body], in_sem.at[0]),
        pltpu.make_async_copy(rs_h, rs6, in_sem.at[1]),
        pltpu.make_async_copy(land_h, land, in_sem.at[2]),
        pltpu.make_async_copy(cnt_h, cnt, in_sem.at[3]),
    ]
    for copy in loads:
        copy.start()

    barrier = pltpu.get_barrier_semaphore()
    for peer in day_peer[1:] + lon_peer[1:]:
        pl.semaphore_signal(barrier, inc=1, device_id=peer, device_id_type=MESH)
    pl.semaphore_wait(barrier, n_day + n_lon - 2)

    fields = (latp, p0p, up)
    kvs = (kv0, kv1, kv2)
    edges = (0, last)

    def plane(rnd, kind, c, side):
        rows = pl.ds(c * CHUNK, CHUNK)
        if kind == 0:
            if rnd == 0:
                src = lat_h.at[edges[side], rows]
            else:
                src = fields[rnd].at[edges[side], pl.ds(PAD + c * CHUNK, CHUNK)]
            dst = vrecv.at[rnd, 1 - side, rows]
        else:
            src = psend.at[rnd, side, rows]
            dst = precv.at[rnd, 1 - side, rows]
        return pltpu.make_async_remote_copy(
            src_ref=src, dst_ref=dst,
            send_sem=plane_ss.at[rnd, kind, c, side], recv_sem=plane_rs.at[rnd, kind, c, 1 - side],
            device_id=sides[side], device_id_type=MESH,
        )

    def column(rnd, kind, c, side):
        return pltpu.make_async_remote_copy(
            src_ref=csend.at[rnd, kind, c], dst_ref=crecv.at[rnd, kind, c, 1 - side],
            send_sem=col_ss.at[rnd, kind, c, side], recv_sem=col_rs.at[rnd, kind, c, 1 - side],
            device_id=beside[side], device_id_type=MESH,
        )

    def unrolled(n, body, carry):
        for i in range(n):
            carry = body(i, carry)
        return carry

    def start_both(copy, rnd, kind, c):
        copy(rnd, kind, c, 0).start()
        copy(rnd, kind, c, 1).start()

    def wait_both(copy, rnd, kind, c):
        copy(rnd, kind, c, 0).wait_recv()
        copy(rnd, kind, c, 1).wait_recv()

    def first_planes(c, carry):
        start_both(plane, 0, 0, c)
        return carry

    lax.fori_loop(0, chunks, first_planes, 0)

    lane = lax.broadcasted_iota(jnp.int32, (GROUP, lons), 1)
    pair = ((lane + 1) & (lons - 1)) >> 1
    lane_block = lax.broadcasted_iota(jnp.int32, (BLOCK, lons), 1)
    at_low = lane_block == 0
    at_high = lane_block == lons - 1
    even = (lane & 1) == 0
    zeros = jnp.zeros((GROUP, lons), jnp.float32)

    def gather(tile, d, b):
        acc = zeros
        for k in range(per_block):
            j = d * groups + b * per_block + k
            acc = jnp.where(pair == j, pltpu.roll(tile[k * GROUP:(k + 1) * GROUP], (2 * j) % lons, 1), acc)
        return acc

    def outer_columns(rnd, kind, c):
        low = crecv[rnd, kind, c, 0]
        high = crecv[rnd, kind, c, 1]
        return jnp.where(even, pltpu.roll(low, 1, 1), pltpu.roll(high, lons - 1, 1))

    def along_lon(x, cols, d, b):
        outer = jnp.concatenate(
            [pltpu.roll(cols, (0 - 2 * (d * groups + b * per_block + k)) % lons, 1) for k in range(per_block)], axis=0
        )
        return jnp.where(at_low, outer, pltpu.roll(x, 1, 1)) + jnp.where(at_high, outer, pltpu.roll(x, lons - 1, 1))

    def own_part(ref, cols, row, b):
        x = [ref[d, pl.ds(PAD + row, BLOCK)] for d in range(days)]
        out = []
        for d in range(days):
            near = ref[d, pl.ds(PAD - 1 + row, BLOCK)] + ref[d, pl.ds(PAD + 1 + row, BLOCK)]
            near = near + along_lon(x[d], cols, d, b)
            if d > 0:
                near = near + x[d - 1]
            if d < last:
                near = near + x[d + 1]
            out.append(rs6[d, pl.ds(row, BLOCK)] * x[d] - near)
        return out

    def send_columns(rnd, kind, c, acc):
        csend[rnd, kind, c] = acc
        start_both(column, rnd, kind, c)

    def first_k(rnd, c, total):
        wait_both(column, rnd, 0, c)
        cols = outer_columns(rnd, 0, c)
        field, kv = fields[rnd], kvs[rnd]

        def partial(b, carry):
            row = pl.multiple_of(c * CHUNK + b * BLOCK, BLOCK)
            out = own_part(field, cols, row, b)
            rows = pl.ds(row, BLOCK)
            psend[rnd, 0, rows] = out[0]
            psend[rnd, 1, rows] = out[last]
            for d in range(1, last):
                kv[d, pl.ds(PAD + row, BLOCK)] = out[d]
            return carry

        unrolled(blocks, partial, 0)
        start_both(plane, rnd, 1, c)
        wait_both(plane, rnd, 0, c)

        def complete(b, carry):
            acc, totals = carry
            row = pl.multiple_of(c * CHUNK + b * BLOCK, BLOCK)
            rows = pl.ds(row, BLOCK)
            wide = pl.ds(PAD + row, BLOCK)
            for d in range(days):
                if d == 0 or d == last:
                    side = 0 if d == 0 else 1
                    tile = psend[rnd, side, rows] - vrecv[rnd, side, rows]
                    kv[d, wide] = tile
                else:
                    tile = kv[d, wide]
                acc = acc + gather(tile, d, b)
                if rnd == 1:
                    p = field[d, wide]
                    totals = (totals[0] + fold(SCALE * tile * tile + weight[d, rows] * p * p),)
                if rnd == 2:
                    w, u = weight[d, rows], field[d, wide]
                    z = p0p[d, wide] - u
                    kz = kv1[d, wide] - tile
                    skz, wz = SCALE * kz, w * z
                    totals = (
                        totals[0] + fold(skz * kz + wz * z),
                        totals[1] + fold(skz * tile + wz * u),
                        totals[2] + fold(SCALE * tile * tile + w * u * u),
                    )
            return acc, totals

        acc, total = unrolled(blocks, complete, (zeros, total))
        send_columns(rnd, 1, c, acc)
        return total

    def fold(x):
        while x.shape[0] > GROUP:
            half = x.shape[0] // 2
            x = x[:half] + x[half:]
        return x

    def second_k(rnd, c, total):
        wait_both(column, rnd, 1, c)
        wait_both(plane, rnd, 1, c)
        cols = outer_columns(rnd, 1, c)
        field, kv = fields[rnd], kvs[rnd]

        def rest(b, carry):
            acc, totals = carry
            row = pl.multiple_of(c * CHUNK + b * BLOCK, BLOCK)
            rows = pl.ds(row, BLOCK)
            wide = pl.ds(PAD + row, BLOCK)
            out = own_part(kv, cols, row, b)
            out[0] = out[0] - (precv[rnd, 0, rows] - field[0, wide])
            out[last] = out[last] - (precv[rnd, 1, rows] - field[last, wide])
            for d in range(days):
                image = SCALE * out[d]
                if rnd == 0:
                    base = sres[d, rows]
                    residual = 0.0 - (image + base)
                    value = residual * inv[d, rows]
                    r0[d, rows] = residual
                    p0p[d, wide] = value
                else:
                    image = image + weight[d, rows] * field[d, wide]
                    if rnd == 1:
                        value = image * inv[d, rows]
                        q0[d, rows] = image
                        up[d, wide] = value
                        p = field[d, wide]
                        y, z = r0[d, rows] - image, p - value
                        totals = (
                            totals[0] + fold(y * p),
                            totals[1] + fold(y * z),
                            totals[2] + fold(y * value),
                            totals[3] + fold(image * value),
                        )
                    else:
                        sres[d, rows] = image
                if rnd < ROUNDS - 1:
                    acc = acc + gather(value, d, b)
            return acc, totals

        acc, total = unrolled(blocks, rest, (zeros, total))
        if rnd < ROUNDS - 1:
            start_both(plane, rnd + 1, 0, c)
            send_columns(rnd + 1, 0, c, acc)
        return total

    def peer_copy(stage, k):
        peers = (lon_peer, day_peer)[stage]
        return pltpu.make_async_remote_copy(
            src_ref=redsend.at[stage], dst_ref=redrecv.at[stage, k],
            send_sem=red_ss.at[stage, k], recv_sem=red_rs.at[stage, k],
            device_id=peers[k], device_id_type=MESH,
        )

    def reduce_start(stage, rows):
        redsend[stage] = rows
        for k in range(1, (n_lon, n_day)[stage]):
            peer_copy(stage, k).start()

    def reduce_wait(stage):
        n = (n_lon, n_day)[stage]
        total = redsend[stage]
        for k in range(1, n):
            peer_copy(stage, k).wait_recv()
        for k in range(1, n):
            total = total + redrecv[stage, k]
        return total

    def as_rows(values):
        row = lax.broadcasted_iota(jnp.int32, (GROUP, lons), 0)
        out = zeros
        for i, v in enumerate(values):
            out = jnp.where(row == i, jnp.sum(v, axis=0, keepdims=True), out)
        return out

    loads[0].wait()
    for ref in (latp, p0p, up, kv0, kv1, kv2):
        for d in range(days):
            ref[d, pl.ds(0, PAD)] = zeros
            ref[d, pl.ds(PAD + lats, PAD)] = zeros

    def first_columns(c, carry):
        def step(b, acc):
            row = pl.multiple_of(c * CHUNK + b * BLOCK, BLOCK)
            for d in range(days):
                acc = acc + gather(latp[d, pl.ds(PAD + row, BLOCK)], d, b)
            return acc

        send_columns(0, 0, c, unrolled(blocks, step, zeros))
        return carry

    lax.fori_loop(0, chunks, first_columns, 0)

    for copy in loads[1:]:
        copy.wait()

    def prepare(b, carry):
        row = pl.multiple_of(b * SMALL, SMALL)
        rows = pl.ds(row, SMALL)
        at = row + lax.broadcasted_iota(jnp.int32, (SMALL, lons), 0)
        near = 6.0 - jnp.where(at == 0, 1.0, 0.0) - jnp.where(at == lats - 1, 1.0, 0.0)
        for d in range(days):
            mask = land[d, rows].astype(jnp.float32)
            w = mask * jnp.exp(latp[d, pl.ds(PAD + row, SMALL)])
            diag = rs6[d, rows] + 6.0
            rs6[d, rows] = diag
            weight[d, rows] = w
            inv[d, rows] = 1.0 / (SCALE * (diag * diag + near) + w)
            sres[d, rows] = w - mask * cnt[d, rows].astype(jnp.float32)
        return carry

    lax.fori_loop(0, lats // SMALL, prepare, 0)

    sums = []
    for rnd in range(ROUNDS):
        start = ((), (zeros,), (zeros,) * 3)[rnd]
        sums += lax.fori_loop(0, chunks, functools.partial(first_k, rnd), start)
        if rnd == 2:
            reduce_start(0, as_rows(sums))
        turn = functools.partial(second_k, rnd)
        if rnd < 2:
            sums += lax.fori_loop(0, chunks, turn, ((), (zeros,) * 4)[rnd])
        else:
            lax.fori_loop(0, chunks - 1, turn, ())
            reduce_start(1, reduce_wait(0))
            turn(chunks - 1, ())

    all_sums = jnp.sum(reduce_wait(1), axis=1, keepdims=True)
    m1, n1, n2, n3, m2, zz, zu, uu = [jnp.broadcast_to(all_sums[i:i + 1], (1, lons)) for i in range(GROUP)]
    extra = n1 / m1
    a0 = 1.0 + extra
    rz1 = n2 - 2.0 * extra * n3 + extra * extra * m2
    beta = rz1 / (m1 + n1)
    zq = n3 - extra * m2
    zhz = zz - 2.0 * extra * zu + extra * extra * uu
    a1 = rz1 / (zhz + 2.0 * beta * zq + beta * beta * m1)
    coefs[0:1] = a0 + a1 * (1.0 + beta)
    coefs[1:2] = a0 * a1

    def drain(c, carry):
        for rnd in range(ROUNDS):
            for kind in range(2):
                for side in range(2):
                    plane(rnd, kind, c, side).wait_send()
                    column(rnd, kind, c, side).wait_send()
        return carry

    lax.fori_loop(0, chunks, drain, 0)
    for stage in range(2):
        for k in range(1, (n_lon, n_day)[stage]):
            peer_copy(stage, k).wait_send()


def solution(mesh):
    names = tuple(mesh.axis_names)
    n_day, n_lon = mesh.shape["day"], mesh.shape["lon"]
    spec = P("day", None, "lon")

    def per_device(latent, range_sq, counts, land):
        days, lats, lons = latent.shape
        chunks = lats // CHUNK
        f32 = jnp.float32
        whole = (days, lats, lons)
        padded = (days, lats + 2 * PAD, lons)
        vmem = pltpu.VMEM
        dma = pltpu.SemaphoreType.DMA
        p0, u, r0, q0, s, coefs = pl.pallas_call(
            functools.partial(kernel, names, n_day, n_lon),
            out_shape=[
                vmem(padded, f32), vmem(padded, f32), vmem(whole, f32), vmem(whole, f32), vmem(whole, f32),
                vmem((2, lons), f32),
            ],
            in_specs=[pl.BlockSpec(memory_space=pl.ANY)] * 4,
            out_specs=[pl.BlockSpec(memory_space=pltpu.VMEM)] * 6,
            scratch_shapes=[
                vmem(padded, f32), vmem(whole, f32), vmem(whole, jnp.int32), vmem(whole, jnp.int32),
                vmem(whole, f32), vmem(whole, f32),
                vmem(padded, f32), vmem(padded, f32), vmem(padded, f32),
                vmem((ROUNDS, 2, lats, lons), f32), vmem((ROUNDS, 2, lats, lons), f32),
                vmem((ROUNDS, 2, lats, lons), f32),
                vmem((ROUNDS, 2, chunks, GROUP, lons), f32), vmem((ROUNDS, 2, chunks, 2, GROUP, lons), f32),
                vmem((2, GROUP, lons), f32), vmem((2, n_lon, GROUP, lons), f32),
                dma((ROUNDS, 2, chunks, 2)), dma((ROUNDS, 2, chunks, 2)),
                dma((ROUNDS, 2, chunks, 2)), dma((ROUNDS, 2, chunks, 2)),
                dma((2, n_lon)), dma((2, n_lon)), dma((4,)),
            ],
            compiler_params=pltpu.CompilerParams(
                collective_id=0, has_side_effects=True, vmem_limit_bytes=44 << 20
            ),
        )(latent, range_sq, counts, land)
        body = slice(PAD, PAD + lats)
        step = coefs[0] * p0[:, body] - coefs[1] * u[:, body]
        residual = r0 - coefs[0] * q0 + coefs[1] * s
        return step, residual

    return jax.shard_map(per_device, mesh=mesh, in_specs=(spec,) * 4, out_specs=(spec, spec), check_vma=False)
```

```python
import functools

import jax
import jax.numpy as jnp
from jax import lax
from jax.experimental import pallas as pl
from jax.experimental.pallas import tpu as pltpu
from jax.sharding import PartitionSpec as P

ROUNDS = 3
SCALE = 0.02
PAD = 8
GROUP = 8
CHUNK = 128
BLOCK = 128
SMALL = 64
HELD = 3
MESH = pl.DeviceIdType.MESH


def kernel(
    names, n_day, n_lon,
    lat_h, rs_h, cnt_h, land_h, p0p, up, r0, q0, sres, coefs,
    latp, rs6, cnt, land, weight, inv, kv0, kv1, kv2,
    psend, vrecv, precv, csend, crecv, redsend, redrecv,
    plane_ss, plane_rs, col_ss, col_rs, red_ss, red_rs, in_sem,
):
    days, lats, lons = rs6.shape
    last = days - 1
    chunks = lats // CHUNK
    groups = CHUNK // GROUP
    blocks = CHUNK // BLOCK
    per_block = BLOCK // GROUP
    me_d = lax.axis_index("day")
    me_l = lax.axis_index("lon")

    def device(day, lon):
        where = {"day": day, "lon": lon}
        return tuple(where[n] for n in names)

    day_peer = [device(lax.rem(me_d + k, n_day), me_l) for k in range(n_day)]
    lon_peer = [device(me_d, lax.rem(me_l + k, n_lon)) for k in range(n_lon)]
    sides = (day_peer[n_day - 1], day_peer[1])
    beside = (lon_peer[n_lon - 1], lon_peer[1])

    body = pl.ds(PAD, lats)
    loads = [
        pltpu.make_async_copy(lat_h, latp.at[:, body], in_sem.at[0]),
        pltpu.make_async_copy(rs_h, rs6, in_sem.at[1]),
        pltpu.make_async_copy(land_h, land, in_sem.at[2]),
        pltpu.make_async_copy(cnt_h, cnt, in_sem.at[3]),
    ]
    barrier = pltpu.get_barrier_semaphore()
    for peer in day_peer[1:] + lon_peer[1:]:
        pl.semaphore_signal(barrier, inc=1, device_id=peer, device_id_type=MESH)
    pl.semaphore_wait(barrier, n_day + n_lon - 2)

    fields = (latp, p0p, up)
    kvs = (kv0, kv1, kv2)
    edges = (0, last)

    def plane(rnd, kind, c, side, size=CHUNK):
        rows = pl.ds(c * CHUNK, size)
        if kind == 0:
            if rnd == 0:
                src = lat_h.at[edges[side], rows]
            else:
                src = fields[rnd].at[edges[side], pl.ds(PAD + c * CHUNK, size)]
            dst = vrecv.at[rnd, 1 - side, rows]
        else:
            src = psend.at[rnd, side, rows]
            dst = precv.at[rnd, 1 - side, rows]
        return pltpu.make_async_remote_copy(
            src_ref=src, dst_ref=dst,
            send_sem=plane_ss.at[rnd, kind, side], recv_sem=plane_rs.at[rnd, kind, c, 1 - side],
            device_id=sides[side], device_id_type=MESH,
        )

    def column(rnd, kind, c, side):
        return pltpu.make_async_remote_copy(
            src_ref=csend.at[rnd, kind, c], dst_ref=crecv.at[rnd, kind, 1 - side, c],
            send_sem=col_ss.at[rnd, kind, side], recv_sem=col_rs.at[rnd, kind, c, 1 - side],
            device_id=beside[side], device_id_type=MESH,
        )

    def unrolled(n, body, carry):
        for i in range(n):
            carry = body(i, carry)
        return carry

    def all_columns(rnd, kind, side):
        return pltpu.make_async_remote_copy(
            src_ref=csend.at[rnd, kind], dst_ref=crecv.at[rnd, kind, 1 - side],
            send_sem=col_ss.at[rnd, kind, side], recv_sem=col_rs.at[rnd, kind, 0, 1 - side],
            device_id=beside[side], device_id_type=MESH,
        )

    def start_both(copy, rnd, kind, c):
        copy(rnd, kind, c, 0).start()
        copy(rnd, kind, c, 1).start()

    def wait_both(copy, rnd, kind, c):
        copy(rnd, kind, c, 0).wait_recv()
        copy(rnd, kind, c, 1).wait_recv()

    def first_planes(c, carry):
        start_both(plane, 0, 0, c)
        return carry

    lax.fori_loop(0, chunks, first_planes, 0)
    for copy in loads:
        copy.start()

    lane = lax.broadcasted_iota(jnp.int32, (GROUP, lons), 1)
    pair = ((lane + 1) & (lons - 1)) >> 1
    lane_block = lax.broadcasted_iota(jnp.int32, (BLOCK, lons), 1)
    at_low = lane_block == 0
    at_high = lane_block == lons - 1
    even = (lane & 1) == 0
    zeros = jnp.zeros((GROUP, lons), jnp.float32)

    def gather(tile, d, b):
        acc = zeros
        for k in range(per_block):
            j = d * groups + b * per_block + k
            acc = jnp.where(pair == j, pltpu.roll(tile[k * GROUP:(k + 1) * GROUP], (2 * j) % lons, 1), acc)
        return acc

    def outer_columns(rnd, kind, c):
        low = crecv[rnd, kind, 0, c]
        high = crecv[rnd, kind, 1, c]
        return jnp.where(even, pltpu.roll(low, 1, 1), pltpu.roll(high, lons - 1, 1))

    def along_lon(x, cols, d, b):
        outer = jnp.concatenate(
            [pltpu.roll(cols, (0 - 2 * (d * groups + b * per_block + k)) % lons, 1) for k in range(per_block)], axis=0
        )
        return jnp.where(at_low, outer, pltpu.roll(x, 1, 1)) + jnp.where(at_high, outer, pltpu.roll(x, lons - 1, 1))

    def own_part(ref, cols, row, b):
        x = [ref[d, pl.ds(PAD + row, BLOCK)] for d in range(days)]
        out = []
        for d in range(days):
            near = ref[d, pl.ds(PAD - 1 + row, BLOCK)] + ref[d, pl.ds(PAD + 1 + row, BLOCK)]
            near = near + along_lon(x[d], cols, d, b)
            if d > 0:
                near = near + x[d - 1]
            if d < last:
                near = near + x[d + 1]
            out.append(rs6[d, pl.ds(row, BLOCK)] * x[d] - near)
        return out

    def send_columns(rnd, kind, c, acc):
        csend[rnd, kind, c] = acc
        start_both(column, rnd, kind, c)

    def first_k(rnd, send, c, total):
        wait_both(column, rnd, 0, c)
        cols = outer_columns(rnd, 0, c)
        field, kv = fields[rnd], kvs[rnd]

        def partial(b, carry):
            row = pl.multiple_of(c * CHUNK + b * BLOCK, BLOCK)
            out = own_part(field, cols, row, b)
            rows = pl.ds(row, BLOCK)
            psend[rnd, 0, rows] = out[0]
            psend[rnd, 1, rows] = out[last]
            for d in range(1, last):
                kv[d, pl.ds(PAD + row, BLOCK)] = out[d]
            return carry

        unrolled(blocks, partial, 0)
        if send:
            start_both(plane, rnd, 1, c)
        wait_both(plane, rnd, 0, c)

        def complete(b, carry):
            acc, totals = carry
            row = pl.multiple_of(c * CHUNK + b * BLOCK, BLOCK)
            rows = pl.ds(row, BLOCK)
            wide = pl.ds(PAD + row, BLOCK)
            for d in range(days):
                if d == 0 or d == last:
                    side = 0 if d == 0 else 1
                    tile = psend[rnd, side, rows] - vrecv[rnd, side, rows]
                    kv[d, wide] = tile
                else:
                    tile = kv[d, wide]
                acc = acc + gather(tile, d, b)
                if rnd == 1:
                    p = field[d, wide]
                    totals = (totals[0] + fold(SCALE * tile * tile + weight[d, rows] * p * p),)
                if rnd == 2:
                    w, u = weight[d, rows], field[d, wide]
                    z = p0p[d, wide] - u
                    kz = kv1[d, wide] - tile
                    skz, wz = SCALE * kz, w * z
                    totals = (
                        totals[0] + fold(skz * kz + wz * z),
                        totals[1] + fold(skz * tile + wz * u),
                        totals[2] + fold(SCALE * tile * tile + w * u * u),
                    )
            return acc, totals

        acc, total = unrolled(blocks, complete, (zeros, total))
        send_columns(rnd, 1, c, acc)
        return total

    def fold(x):
        while x.shape[0] > GROUP:
            half = x.shape[0] // 2
            x = x[:half] + x[half:]
        return x

    def second_k(rnd, c, total):
        wait_both(column, rnd, 1, c)
        wait_both(plane, rnd, 1, c)
        cols = outer_columns(rnd, 1, c)
        field, kv = fields[rnd], kvs[rnd]

        def rest(b, carry):
            acc, totals = carry
            row = pl.multiple_of(c * CHUNK + b * BLOCK, BLOCK)
            rows = pl.ds(row, BLOCK)
            wide = pl.ds(PAD + row, BLOCK)
            out = own_part(kv, cols, row, b)
            out[0] = out[0] - (precv[rnd, 0, rows] - field[0, wide])
            out[last] = out[last] - (precv[rnd, 1, rows] - field[last, wide])
            for d in range(days):
                image = SCALE * out[d]
                if rnd == 0:
                    base = sres[d, rows]
                    residual = 0.0 - (image + base)
                    value = residual * inv[d, rows]
                    r0[d, rows] = residual
                    p0p[d, wide] = value
                else:
                    image = image + weight[d, rows] * field[d, wide]
                    if rnd == 1:
                        value = image * inv[d, rows]
                        q0[d, rows] = image
                        up[d, wide] = value
                        p = field[d, wide]
                        y, z = r0[d, rows] - image, p - value
                        totals = (
                            totals[0] + fold(y * p),
                            totals[1] + fold(y * z),
                            totals[2] + fold(y * value),
                            totals[3] + fold(image * value),
                        )
                    else:
                        sres[d, rows] = image
                if rnd < ROUNDS - 1:
                    acc = acc + gather(value, d, b)
            return acc, totals

        acc, total = unrolled(blocks, rest, (zeros, total))
        if rnd < ROUNDS - 1:
            start_both(plane, rnd + 1, 0, c)
            send_columns(rnd + 1, 0, c, acc)
        return total

    def peer_copy(stage, k):
        peers = (day_peer, lon_peer)[stage]
        return pltpu.make_async_remote_copy(
            src_ref=redsend.at[stage], dst_ref=redrecv.at[stage, k],
            send_sem=red_ss.at[stage, k], recv_sem=red_rs.at[stage, k],
            device_id=peers[k], device_id_type=MESH,
        )

    def reduce_start(stage, rows):
        redsend[stage] = rows
        for k in range(1, (n_day, n_lon)[stage]):
            peer_copy(stage, k).start()

    def reduce_wait(stage):
        n = (n_day, n_lon)[stage]
        total = redsend[stage]
        for k in range(1, n):
            peer_copy(stage, k).wait_recv()
        for k in range(1, n):
            total = total + redrecv[stage, k]
        return total

    def as_rows(values):
        row = lax.broadcasted_iota(jnp.int32, (GROUP, lons), 0)
        out = zeros
        for i, v in enumerate(values):
            out = jnp.where(row == i, jnp.sum(v, axis=0, keepdims=True), out)
        return out

    loads[0].wait()
    for ref in (latp, p0p, up, kv0, kv1, kv2):
        for d in range(days):
            ref[d, pl.ds(0, PAD)] = zeros
            ref[d, pl.ds(PAD + lats, PAD)] = zeros

    def first_columns(c, carry):
        def step(b, acc):
            row = pl.multiple_of(c * CHUNK + b * BLOCK, BLOCK)
            for d in range(days):
                acc = acc + gather(latp[d, pl.ds(PAD + row, BLOCK)], d, b)
            return acc

        send_columns(0, 0, c, unrolled(blocks, step, zeros))
        return carry

    lax.fori_loop(0, chunks, first_columns, 0)

    for copy in loads[1:]:
        copy.wait()

    def prepare(b, carry):
        row = pl.multiple_of(b * SMALL, SMALL)
        rows = pl.ds(row, SMALL)
        at = row + lax.broadcasted_iota(jnp.int32, (SMALL, lons), 0)
        near = 6.0 - jnp.where(at == 0, 1.0, 0.0) - jnp.where(at == lats - 1, 1.0, 0.0)
        for d in range(days):
            mask = land[d, rows].astype(jnp.float32)
            w = mask * jnp.exp(latp[d, pl.ds(PAD + row, SMALL)])
            diag = rs6[d, rows] + 6.0
            rs6[d, rows] = diag
            weight[d, rows] = w
            inv[d, rows] = 1.0 / (SCALE * (diag * diag + near) + w)
            sres[d, rows] = w - mask * cnt[d, rows].astype(jnp.float32)
        return carry

    lax.fori_loop(0, lats // SMALL, prepare, 0)

    sums = []
    for rnd in range(ROUNDS - 1):
        sums += lax.fori_loop(0, chunks, functools.partial(first_k, rnd, True), ((), (zeros,))[rnd])
        sums += lax.fori_loop(0, chunks, functools.partial(second_k, rnd), ((), (zeros,) * 4)[rnd])

    rnd = ROUNDS - 1
    total = lax.fori_loop(0, chunks - HELD, functools.partial(first_k, rnd, True), (zeros,) * 3)
    sums += lax.fori_loop(chunks - HELD, chunks, functools.partial(first_k, rnd, False), total)
    reduce_start(0, as_rows(sums))
    for c in range(chunks - HELD, chunks):
        start_both(plane, rnd, 1, c)
    lax.fori_loop(0, chunks - HELD, functools.partial(second_k, rnd), ())
    reduce_start(1, reduce_wait(0))
    lax.fori_loop(chunks - HELD, chunks, functools.partial(second_k, rnd), ())

    for rnd in range(ROUNDS):
        for kind in range(2):
            for side in range(2):
                plane(rnd, kind, 0, side, lats).wait_send()
                all_columns(rnd, kind, side).wait_send()
    for k in range(1, n_day):
        peer_copy(0, k).wait_send()

    all_sums = jnp.sum(reduce_wait(1), axis=1, keepdims=True)
    m1, n1, n2, n3, m2, zz, zu, uu = [jnp.broadcast_to(all_sums[i:i + 1], (1, lons)) for i in range(GROUP)]
    extra = n1 / m1
    a0 = 1.0 + extra
    rz1 = n2 - 2.0 * extra * n3 + extra * extra * m2
    beta = rz1 / (m1 + n1)
    zq = n3 - extra * m2
    zhz = zz - 2.0 * extra * zu + extra * extra * uu
    a1 = rz1 / (zhz + 2.0 * beta * zq + beta * beta * m1)
    coefs[0:1] = a0 + a1 * (1.0 + beta)
    coefs[1:2] = a0 * a1

    for k in range(1, n_lon):
        peer_copy(1, k).wait_send()


def solution(mesh):
    names = tuple(mesh.axis_names)
    n_day, n_lon = mesh.shape["day"], mesh.shape["lon"]
    spec = P("day", None, "lon")

    def per_device(latent, range_sq, counts, land):
        days, lats, lons = latent.shape
        chunks = lats // CHUNK
        f32 = jnp.float32
        whole = (days, lats, lons)
        padded = (days, lats + 2 * PAD, lons)
        vmem = pltpu.VMEM
        dma = pltpu.SemaphoreType.DMA
        p0, u, r0, q0, s, coefs = pl.pallas_call(
            functools.partial(kernel, names, n_day, n_lon),
            out_shape=[
                vmem(padded, f32), vmem(padded, f32), vmem(whole, f32), vmem(whole, f32), vmem(whole, f32),
                vmem((2, lons), f32),
            ],
            in_specs=[pl.BlockSpec(memory_space=pl.ANY)] * 4,
            out_specs=[pl.BlockSpec(memory_space=pltpu.VMEM)] * 6,
            scratch_shapes=[
                vmem(padded, f32), vmem(whole, f32), vmem(whole, jnp.int32), vmem(whole, jnp.int32),
                vmem(whole, f32), vmem(whole, f32),
                vmem(padded, f32), vmem(padded, f32), vmem(padded, f32),
                vmem((ROUNDS, 2, lats, lons), f32), vmem((ROUNDS, 2, lats, lons), f32),
                vmem((ROUNDS, 2, lats, lons), f32),
                vmem((ROUNDS, 2, chunks, GROUP, lons), f32), vmem((ROUNDS, 2, 2, chunks, GROUP, lons), f32),
                vmem((2, GROUP, lons), f32), vmem((2, n_lon, GROUP, lons), f32),
                dma((ROUNDS, 2, 2)), dma((ROUNDS, 2, chunks, 2)),
                dma((ROUNDS, 2, 2)), dma((ROUNDS, 2, chunks, 2)),
                dma((2, n_lon)), dma((2, n_lon)), dma((4,)),
            ],
            compiler_params=pltpu.CompilerParams(
                collective_id=0, has_side_effects=True, vmem_limit_bytes=44 << 20
            ),
        )(latent, range_sq, counts, land)
        body = slice(PAD, PAD + lats)
        step = coefs[0] * p0[:, body] - coefs[1] * u[:, body]
        residual = r0 - coefs[0] * q0 + coefs[1] * s
        return step, residual

    return jax.shard_map(per_device, mesh=mesh, in_specs=(spec,) * 4, out_specs=(spec, spec), check_vma=False)
```

```python
import functools

import jax
import jax.numpy as jnp
from jax import lax
from jax.experimental import pallas as pl
from jax.experimental.pallas import tpu as pltpu
from jax.sharding import PartitionSpec as P

ROUNDS = 3
SCALE = 0.02
PAD = 8
GROUP = 8
CHUNK = 128
MERGE = ((2, 2), (2, 2), (1, 2))
TURN = 2
BLOCK = 128
SMALL = 64
HELD = 2
MESH = pl.DeviceIdType.MESH


def kernel(
    names, n_day, n_lon,
    lat_h, rs_h, cnt_h, land_h, p0p, up, r0, q0, sres, coefs,
    latp, rs6, cnt, land, weight, inv, kv0, kv1, kv2,
    psend, vrecv, precv, csend, crecv, redsend, redrecv,
    plane_ss, plane_rs, col_ss, col_rs, red_ss, red_rs, in_sem,
):
    days, lats, lons = rs6.shape
    last = days - 1
    chunks = lats // CHUNK
    groups = CHUNK // GROUP
    blocks = CHUNK // BLOCK
    per_block = BLOCK // GROUP
    me_d = lax.axis_index("day")
    me_l = lax.axis_index("lon")

    def device(day, lon):
        where = {"day": day, "lon": lon}
        return tuple(where[n] for n in names)

    day_peer = [device(lax.rem(me_d + k, n_day), me_l) for k in range(n_day)]
    lon_peer = [device(me_d, lax.rem(me_l + k, n_lon)) for k in range(n_lon)]
    sides = (day_peer[n_day - 1], day_peer[1])
    beside = (lon_peer[n_lon - 1], lon_peer[1])

    body = pl.ds(PAD, lats)
    loads = [
        pltpu.make_async_copy(lat_h, latp.at[:, body], in_sem.at[0]),
        pltpu.make_async_copy(rs_h, rs6, in_sem.at[1]),
        pltpu.make_async_copy(land_h, land, in_sem.at[2]),
        pltpu.make_async_copy(cnt_h, cnt, in_sem.at[3]),
    ]
    loads[0].start()
    barrier = pltpu.get_barrier_semaphore()
    for peer in day_peer[1:] + lon_peer[1:]:
        pl.semaphore_signal(barrier, inc=1, device_id=peer, device_id_type=MESH)
    pl.semaphore_wait(barrier, n_day + n_lon - 2)

    fields = (latp, p0p, up)
    kvs = (kv0, kv1, kv2)
    edges = (0, last)

    def plane(rnd, kind, c, side, size=None):
        if size is None:
            size = CHUNK * MERGE[rnd][kind]
        rows = pl.ds(c * CHUNK, size)
        if kind == 0:
            if rnd == 0:
                src = lat_h.at[edges[side], rows]
            else:
                src = fields[rnd].at[edges[side], pl.ds(PAD + c * CHUNK, size)]
            dst = vrecv.at[rnd, 1 - side, rows]
        else:
            src = psend.at[rnd, side, rows]
            dst = precv.at[rnd, 1 - side, rows]
        return pltpu.make_async_remote_copy(
            src_ref=src, dst_ref=dst,
            send_sem=plane_ss.at[rnd, kind, side], recv_sem=plane_rs.at[rnd, kind, c, 1 - side],
            device_id=sides[side], device_id_type=MESH,
        )

    def column(rnd, kind, c, side):
        return pltpu.make_async_remote_copy(
            src_ref=csend.at[rnd, kind, c], dst_ref=crecv.at[rnd, kind, 1 - side, c],
            send_sem=col_ss.at[rnd, kind, side], recv_sem=col_rs.at[rnd, kind, c, 1 - side],
            device_id=beside[side], device_id_type=MESH,
        )

    def unrolled(n, body, carry):
        for i in range(n):
            carry = body(i, carry)
        return carry

    def all_columns(rnd, kind, side):
        return pltpu.make_async_remote_copy(
            src_ref=csend.at[rnd, kind], dst_ref=crecv.at[rnd, kind, 1 - side],
            send_sem=col_ss.at[rnd, kind, side], recv_sem=col_rs.at[rnd, kind, 0, 1 - side],
            device_id=beside[side], device_id_type=MESH,
        )

    def start_both(copy, rnd, kind, c):
        copy(rnd, kind, c, 0).start()
        copy(rnd, kind, c, 1).start()

    def wait_both(copy, rnd, kind, c):
        copy(rnd, kind, c, 0).wait_recv()
        copy(rnd, kind, c, 1).wait_recv()

    for c in range(0, chunks, MERGE[0][0]):
        start_both(plane, 0, 0, c)
    for copy in loads[1:]:
        copy.start()

    lane = lax.broadcasted_iota(jnp.int32, (GROUP, lons), 1)
    pair = ((lane + 1) & (lons - 1)) >> 1
    lane_block = lax.broadcasted_iota(jnp.int32, (BLOCK, lons), 1)
    at_low = lane_block == 0
    at_high = lane_block == lons - 1
    even = (lane & 1) == 0
    zeros = jnp.zeros((GROUP, lons), jnp.float32)

    def gather(tile, d, b):
        acc = zeros
        for k in range(per_block):
            j = d * groups + b * per_block + k
            acc = jnp.where(pair == j, pltpu.roll(tile[k * GROUP:(k + 1) * GROUP], (2 * j) % lons, 1), acc)
        return acc

    def outer_columns(rnd, kind, c):
        low = crecv[rnd, kind, 0, c]
        high = crecv[rnd, kind, 1, c]
        return jnp.where(even, pltpu.roll(low, 1, 1), pltpu.roll(high, lons - 1, 1))

    def along_lon(x, cols, d, b):
        outer = jnp.concatenate(
            [pltpu.roll(cols, (0 - 2 * (d * groups + b * per_block + k)) % lons, 1) for k in range(per_block)], axis=0
        )
        return jnp.where(at_low, outer, pltpu.roll(x, 1, 1)) + jnp.where(at_high, outer, pltpu.roll(x, lons - 1, 1))

    def own_part(ref, cols, row, b):
        x = [ref[d, pl.ds(PAD + row, BLOCK)] for d in range(days)]
        out = []
        for d in range(days):
            near = ref[d, pl.ds(PAD - 1 + row, BLOCK)] + ref[d, pl.ds(PAD + 1 + row, BLOCK)]
            near = near + along_lon(x[d], cols, d, b)
            if d > 0:
                near = near + x[d - 1]
            if d < last:
                near = near + x[d + 1]
            out.append(rs6[d, pl.ds(row, BLOCK)] * x[d] - near)
        return out

    def send_columns(rnd, kind, c, acc):
        csend[rnd, kind, c] = acc
        start_both(column, rnd, kind, c)

    def first_part(rnd, c):
        wait_both(column, rnd, 0, c)
        cols = outer_columns(rnd, 0, c)
        field, kv = fields[rnd], kvs[rnd]

        def partial(b, carry):
            row = pl.multiple_of(c * CHUNK + b * BLOCK, BLOCK)
            out = own_part(field, cols, row, b)
            rows = pl.ds(row, BLOCK)
            psend[rnd, 0, rows] = out[0]
            psend[rnd, 1, rows] = out[last]
            for d in range(1, last):
                kv[d, pl.ds(PAD + row, BLOCK)] = out[d]
            return carry

        unrolled(blocks, partial, 0)

    def first_rest(rnd, c, total):
        if MERGE[rnd][0] == 1:
            wait_both(plane, rnd, 0, c)
        field, kv = fields[rnd], kvs[rnd]

        def complete(b, carry):
            acc, totals = carry
            row = pl.multiple_of(c * CHUNK + b * BLOCK, BLOCK)
            rows = pl.ds(row, BLOCK)
            wide = pl.ds(PAD + row, BLOCK)
            for d in range(days):
                if d == 0 or d == last:
                    side = 0 if d == 0 else 1
                    tile = psend[rnd, side, rows] - vrecv[rnd, side, rows]
                    kv[d, wide] = tile
                else:
                    tile = kv[d, wide]
                acc = acc + gather(tile, d, b)
                if rnd == 1:
                    p = field[d, wide]
                    totals = (totals[0] + fold(SCALE * tile * tile + weight[d, rows] * p * p),)
                if rnd == 2:
                    w, u = weight[d, rows], field[d, wide]
                    z = p0p[d, wide] - u
                    kz = kv1[d, wide] - tile
                    skz, wz = SCALE * kz, w * z
                    totals = (
                        totals[0] + fold(skz * kz + wz * z),
                        totals[1] + fold(skz * tile + wz * u),
                        totals[2] + fold(SCALE * tile * tile + w * u * u),
                    )
            return acc, totals

        acc, total = unrolled(blocks, complete, (zeros, total))
        send_columns(rnd, 1, c, acc)
        return total

    def first_k(rnd, send, m, total):
        c = m * TURN

        def part(h, carry):
            first_part(rnd, c + h)
            return carry

        lax.fori_loop(0, TURN, part, 0)
        if send:
            start_both(plane, rnd, 1, c)
        if MERGE[rnd][0] == TURN:
            wait_both(plane, rnd, 0, c)
        return lax.fori_loop(0, TURN, lambda h, t: first_rest(rnd, c + h, t), total)

    def fold(x):
        while x.shape[0] > GROUP:
            half = x.shape[0] // 2
            x = x[:half] + x[half:]
        return x

    def second_part(rnd, c, total):
        wait_both(column, rnd, 1, c)
        cols = outer_columns(rnd, 1, c)
        field, kv = fields[rnd], kvs[rnd]

        def rest(b, carry):
            acc, totals = carry
            row = pl.multiple_of(c * CHUNK + b * BLOCK, BLOCK)
            rows = pl.ds(row, BLOCK)
            wide = pl.ds(PAD + row, BLOCK)
            out = own_part(kv, cols, row, b)
            out[0] = out[0] - (precv[rnd, 0, rows] - field[0, wide])
            out[last] = out[last] - (precv[rnd, 1, rows] - field[last, wide])
            for d in range(days):
                image = SCALE * out[d]
                if rnd == 0:
                    base = sres[d, rows]
                    residual = 0.0 - (image + base)
                    value = residual * inv[d, rows]
                    r0[d, rows] = residual
                    p0p[d, wide] = value
                else:
                    image = image + weight[d, rows] * field[d, wide]
                    if rnd == 1:
                        value = image * inv[d, rows]
                        q0[d, rows] = image
                        up[d, wide] = value
                        p = field[d, wide]
                        y, z = r0[d, rows] - image, p - value
                        totals = (
                            totals[0] + fold(y * p),
                            totals[1] + fold(y * z),
                            totals[2] + fold(y * value),
                            totals[3] + fold(image * value),
                        )
                    else:
                        sres[d, rows] = image
                if rnd < ROUNDS - 1:
                    acc = acc + gather(value, d, b)
            return acc, totals

        acc, total = unrolled(blocks, rest, (zeros, total))
        if rnd < ROUNDS - 1:
            if MERGE[rnd + 1][0] == 1:
                start_both(plane, rnd + 1, 0, c)
            send_columns(rnd + 1, 0, c, acc)
        return total

    def second_k(rnd, m, total):
        c = m * TURN
        wait_both(plane, rnd, 1, c)
        total = lax.fori_loop(0, TURN, lambda h, t: second_part(rnd, c + h, t), total)
        if rnd < ROUNDS - 1 and MERGE[rnd + 1][0] == TURN:
            start_both(plane, rnd + 1, 0, c)
        return total

    def peer_copy(stage, k):
        peers = (day_peer, lon_peer)[stage]
        return pltpu.make_async_remote_copy(
            src_ref=redsend.at[stage], dst_ref=redrecv.at[stage, k],
            send_sem=red_ss.at[stage, k], recv_sem=red_rs.at[stage, k],
            device_id=peers[k], device_id_type=MESH,
        )

    def reduce_start(stage, rows):
        redsend[stage] = rows
        for k in range(1, (n_day, n_lon)[stage]):
            peer_copy(stage, k).start()

    def reduce_wait(stage):
        n = (n_day, n_lon)[stage]
        total = redsend[stage]
        for k in range(1, n):
            peer_copy(stage, k).wait_recv()
        for k in range(1, n):
            total = total + redrecv[stage, k]
        return total

    def as_rows(values):
        row = lax.broadcasted_iota(jnp.int32, (GROUP, lons), 0)
        out = zeros
        for i, v in enumerate(values):
            out = jnp.where(row == i, jnp.sum(v, axis=0, keepdims=True), out)
        return out

    loads[0].wait()
    for ref in (latp, p0p, up, kv0, kv1, kv2):
        for d in range(days):
            ref[d, pl.ds(0, PAD)] = zeros
            ref[d, pl.ds(PAD + lats, PAD)] = zeros

    def first_columns(c, carry):
        def step(b, acc):
            row = pl.multiple_of(c * CHUNK + b * BLOCK, BLOCK)
            for d in range(days):
                acc = acc + gather(latp[d, pl.ds(PAD + row, BLOCK)], d, b)
            return acc

        send_columns(0, 0, c, unrolled(blocks, step, zeros))
        return carry

    lax.fori_loop(0, chunks, first_columns, 0)

    for copy in loads[1:]:
        copy.wait()

    def prepare(b, carry):
        row = pl.multiple_of(b * SMALL, SMALL)
        rows = pl.ds(row, SMALL)
        at = row + lax.broadcasted_iota(jnp.int32, (SMALL, lons), 0)
        near = 6.0 - jnp.where(at == 0, 1.0, 0.0) - jnp.where(at == lats - 1, 1.0, 0.0)
        for d in range(days):
            mask = land[d, rows].astype(jnp.float32)
            w = mask * jnp.exp(latp[d, pl.ds(PAD + row, SMALL)])
            diag = rs6[d, rows] + 6.0
            rs6[d, rows] = diag
            weight[d, rows] = w
            inv[d, rows] = 1.0 / (SCALE * (diag * diag + near) + w)
            sres[d, rows] = w - mask * cnt[d, rows].astype(jnp.float32)
        return carry

    lax.fori_loop(0, lats // SMALL, prepare, 0)

    turns = chunks // TURN
    sums = []
    for rnd in range(ROUNDS - 1):
        sums += lax.fori_loop(0, turns, functools.partial(first_k, rnd, True), ((), (zeros,))[rnd])
        sums += lax.fori_loop(0, turns, functools.partial(second_k, rnd), ((), (zeros,) * 4)[rnd])

    rnd = ROUNDS - 1
    total = lax.fori_loop(0, turns - HELD, functools.partial(first_k, rnd, True), (zeros,) * 3)
    sums += lax.fori_loop(turns - HELD, turns, functools.partial(first_k, rnd, False), total)
    reduce_start(0, as_rows(sums))
    for c in range(turns - HELD, turns):
        start_both(plane, rnd, 1, c * TURN)
    lax.fori_loop(0, turns - HELD, functools.partial(second_k, rnd), ())
    reduce_start(1, reduce_wait(0))
    lax.fori_loop(turns - HELD, turns, functools.partial(second_k, rnd), ())

    for rnd in range(ROUNDS):
        for kind in range(2):
            for side in range(2):
                plane(rnd, kind, 0, side, lats).wait_send()
                all_columns(rnd, kind, side).wait_send()
    for k in range(1, n_day):
        peer_copy(0, k).wait_send()

    all_sums = jnp.sum(reduce_wait(1), axis=1, keepdims=True)
    m1, n1, n2, n3, m2, zz, zu, uu = [jnp.broadcast_to(all_sums[i:i + 1], (1, lons)) for i in range(GROUP)]
    extra = n1 / m1
    a0 = 1.0 + extra
    rz1 = n2 - 2.0 * extra * n3 + extra * extra * m2
    beta = rz1 / (m1 + n1)
    zq = n3 - extra * m2
    zhz = zz - 2.0 * extra * zu + extra * extra * uu
    a1 = rz1 / (zhz + 2.0 * beta * zq + beta * beta * m1)
    coefs[0:1] = a0 + a1 * (1.0 + beta)
    coefs[1:2] = a0 * a1

    for k in range(1, n_lon):
        peer_copy(1, k).wait_send()


def solution(mesh):
    names = tuple(mesh.axis_names)
    n_day, n_lon = mesh.shape["day"], mesh.shape["lon"]
    spec = P("day", None, "lon")

    def per_device(latent, range_sq, counts, land):
        days, lats, lons = latent.shape
        chunks = lats // CHUNK
        f32 = jnp.float32
        whole = (days, lats, lons)
        padded = (days, lats + 2 * PAD, lons)
        vmem = pltpu.VMEM
        dma = pltpu.SemaphoreType.DMA
        p0, u, r0, q0, s, coefs = pl.pallas_call(
            functools.partial(kernel, names, n_day, n_lon),
            out_shape=[
                vmem(padded, f32), vmem(padded, f32), vmem(whole, f32), vmem(whole, f32), vmem(whole, f32),
                vmem((2, lons), f32),
            ],
            in_specs=[pl.BlockSpec(memory_space=pl.ANY)] * 4,
            out_specs=[pl.BlockSpec(memory_space=pltpu.VMEM)] * 6,
            scratch_shapes=[
                vmem(padded, f32), vmem(whole, f32), vmem(whole, jnp.int32), vmem(whole, jnp.int32),
                vmem(whole, f32), vmem(whole, f32),
                vmem(padded, f32), vmem(padded, f32), vmem(padded, f32),
                vmem((ROUNDS, 2, lats, lons), f32), vmem((ROUNDS, 2, lats, lons), f32),
                vmem((ROUNDS, 2, lats, lons), f32),
                vmem((ROUNDS, 2, chunks, GROUP, lons), f32), vmem((ROUNDS, 2, 2, chunks, GROUP, lons), f32),
                vmem((2, GROUP, lons), f32), vmem((2, n_lon, GROUP, lons), f32),
                dma((ROUNDS, 2, 2)), dma((ROUNDS, 2, chunks, 2)),
                dma((ROUNDS, 2, 2)), dma((ROUNDS, 2, chunks, 2)),
                dma((2, n_lon)), dma((2, n_lon)), dma((4,)),
            ],
            compiler_params=pltpu.CompilerParams(
                collective_id=0, has_side_effects=True, vmem_limit_bytes=44 << 20
            ),
        )(latent, range_sq, counts, land)
        body = slice(PAD, PAD + lats)
        step = coefs[0] * p0[:, body] - coefs[1] * u[:, body]
        residual = r0 - coefs[0] * q0 + coefs[1] * s
        return step, residual

    return jax.shard_map(per_device, mesh=mesh, in_specs=(spec,) * 4, out_specs=(spec, spec), check_vma=False)
```

```python
import functools

import jax
import jax.numpy as jnp
from jax import lax
from jax.experimental import pallas as pl
from jax.experimental.pallas import tpu as pltpu
from jax.sharding import PartitionSpec as P

ROUNDS = 3
SCALE = 0.02
PAD = 8
GROUP = 8
CHUNK = 128
MERGE = ((2, 2), (2, 2), (1, 2))
TURN = 2
BLOCK = 128
SMALL = 64
HELD = 2
MESH = pl.DeviceIdType.MESH


def kernel(
    names, n_day, n_lon,
    lat_h, rs_h, cnt_h, land_h, p0p, up, r0, q0, sres, coefs,
    latp, rs6, cnt, land, weight, inv, kv0, kv1, kv2,
    psend, vrecv, precv, csend, crecv, redsend, redrecv,
    plane_ss, plane_rs, col_ss, col_rs, red_ss, red_rs, in_sem,
):
    days, lats, lons = rs6.shape
    last = days - 1
    chunks = lats // CHUNK
    groups = CHUNK // GROUP
    blocks = CHUNK // BLOCK
    per_block = BLOCK // GROUP
    me_d = lax.axis_index("day")
    me_l = lax.axis_index("lon")

    def device(day, lon):
        where = {"day": day, "lon": lon}
        return tuple(where[n] for n in names)

    day_peer = [device(lax.rem(me_d + k, n_day), me_l) for k in range(n_day)]
    lon_peer = [device(me_d, lax.rem(me_l + k, n_lon)) for k in range(n_lon)]
    sides = (day_peer[n_day - 1], day_peer[1])
    beside = (lon_peer[n_lon - 1], lon_peer[1])

    body = pl.ds(PAD, lats)
    loads = [
        pltpu.make_async_copy(lat_h, latp.at[:, body], in_sem.at[0]),
        pltpu.make_async_copy(rs_h, rs6, in_sem.at[1]),
        pltpu.make_async_copy(land_h, land, in_sem.at[2]),
        pltpu.make_async_copy(cnt_h, cnt, in_sem.at[3]),
    ]
    loads[0].start()
    barrier = pltpu.get_barrier_semaphore()
    for peer in day_peer[1:] + lon_peer[1:]:
        pl.semaphore_signal(barrier, inc=1, device_id=peer, device_id_type=MESH)
    pl.semaphore_wait(barrier, n_day + n_lon - 2)

    fields = (latp, p0p, up)
    kvs = (kv0, kv1, kv2)
    edges = (0, last)

    def slot(rnd, c, merge):
        at = c // merge if isinstance(c, int) else lax.div(c, merge)
        return at + (chunks if rnd == 1 else 0)

    def plane(rnd, kind, c, side):
        size = CHUNK * MERGE[rnd][kind]
        rows = pl.ds(c * CHUNK, size)
        if kind == 0:
            if rnd == 0:
                src = lat_h.at[edges[side], rows]
            else:
                src = fields[rnd].at[edges[side], pl.ds(PAD + c * CHUNK, size)]
            dst = vrecv.at[rnd, 1 - side, rows]
        else:
            src = psend.at[rnd, side, rows]
            dst = precv.at[rnd, 1 - side, rows]
        return pltpu.make_async_remote_copy(
            src_ref=src, dst_ref=dst,
            send_sem=plane_ss.at[kind], recv_sem=plane_rs.at[kind, slot(rnd, c, MERGE[rnd][kind]), 1 - side],
            device_id=sides[side], device_id_type=MESH,
        )

    def column(rnd, kind, m, side):
        tiles = pl.ds(0, chunks) if rnd == kind == 0 else pl.ds(m * TURN, TURN)
        return pltpu.make_async_remote_copy(
            src_ref=csend.at[rnd, kind, tiles], dst_ref=crecv.at[1 - side, rnd, kind, tiles],
            send_sem=col_ss.at[side], recv_sem=col_rs.at[kind, m + (chunks // TURN if rnd == 1 else 0), 1 - side],
            device_id=beside[side], device_id_type=MESH,
        )

    def unrolled(n, body, carry):
        for i in range(n):
            carry = body(i, carry)
        return carry

    def start_both(copy, rnd, kind, c):
        copy(rnd, kind, c, 0).start()
        copy(rnd, kind, c, 1).start()

    def wait_both(copy, rnd, kind, c):
        copy(rnd, kind, c, 0).wait_recv()
        copy(rnd, kind, c, 1).wait_recv()

    for c in range(0, chunks, MERGE[0][0]):
        start_both(plane, 0, 0, c)
    for copy in loads[1:]:
        copy.start()

    lane = lax.broadcasted_iota(jnp.int32, (GROUP, lons), 1)
    pair = ((lane + 1) & (lons - 1)) >> 1
    lane_block = lax.broadcasted_iota(jnp.int32, (BLOCK, lons), 1)
    at_low = lane_block == 0
    at_high = lane_block == lons - 1
    even = (lane & 1) == 0
    zeros = jnp.zeros((GROUP, lons), jnp.float32)

    def gather(tile, d, b):
        acc = zeros
        for k in range(per_block):
            j = d * groups + b * per_block + k
            acc = jnp.where(pair == j, pltpu.roll(tile[k * GROUP:(k + 1) * GROUP], (2 * j) % lons, 1), acc)
        return acc

    def outer_columns(rnd, kind, c):
        low = crecv[0, rnd, kind, c]
        high = crecv[1, rnd, kind, c]
        return jnp.where(even, pltpu.roll(low, 1, 1), pltpu.roll(high, lons - 1, 1))

    def along_lon(x, cols, d, b):
        outer = jnp.concatenate(
            [pltpu.roll(cols, (0 - 2 * (d * groups + b * per_block + k)) % lons, 1) for k in range(per_block)], axis=0
        )
        return jnp.where(at_low, outer, pltpu.roll(x, 1, 1)) + jnp.where(at_high, outer, pltpu.roll(x, lons - 1, 1))

    def own_part(ref, cols, row, b):
        x = [ref[d, pl.ds(PAD + row, BLOCK)] for d in range(days)]
        out = []
        for d in range(days):
            near = ref[d, pl.ds(PAD - 1 + row, BLOCK)] + ref[d, pl.ds(PAD + 1 + row, BLOCK)]
            near = near + along_lon(x[d], cols, d, b)
            if d > 0:
                near = near + x[d - 1]
            if d < last:
                near = near + x[d + 1]
            out.append(rs6[d, pl.ds(row, BLOCK)] * x[d] - near)
        return out

    def first_part(rnd, c):
        cols = outer_columns(rnd, 0, c)
        field, kv = fields[rnd], kvs[rnd]

        def partial(b, carry):
            row = pl.multiple_of(c * CHUNK + b * BLOCK, BLOCK)
            out = own_part(field, cols, row, b)
            rows = pl.ds(row, BLOCK)
            psend[rnd, 0, rows] = out[0]
            psend[rnd, 1, rows] = out[last]
            for d in range(1, last):
                kv[d, pl.ds(PAD + row, BLOCK)] = out[d]
            return carry

        unrolled(blocks, partial, 0)

    def first_rest(rnd, c, total):
        if MERGE[rnd][0] == 1:
            wait_both(plane, rnd, 0, c)
        field, kv = fields[rnd], kvs[rnd]

        def complete(b, carry):
            acc, totals = carry
            row = pl.multiple_of(c * CHUNK + b * BLOCK, BLOCK)
            rows = pl.ds(row, BLOCK)
            wide = pl.ds(PAD + row, BLOCK)
            for d in range(days):
                if d == 0 or d == last:
                    side = 0 if d == 0 else 1
                    tile = psend[rnd, side, rows] - vrecv[rnd, side, rows]
                    kv[d, wide] = tile
                else:
                    tile = kv[d, wide]
                acc = acc + gather(tile, d, b)
                if rnd == 1:
                    p = field[d, wide]
                    totals = (totals[0] + fold(SCALE * tile * tile + weight[d, rows] * p * p),)
                if rnd == 2:
                    w, u = weight[d, rows], field[d, wide]
                    z = p0p[d, wide] - u
                    kz = kv1[d, wide] - tile
                    skz, wz = SCALE * kz, w * z
                    totals = (
                        totals[0] + fold(skz * kz + wz * z),
                        totals[1] + fold(skz * tile + wz * u),
                        totals[2] + fold(SCALE * tile * tile + w * u * u),
                    )
            return acc, totals

        acc, total = unrolled(blocks, complete, (zeros, total))
        csend[rnd, 1, c] = acc
        return total

    def first_k(rnd, send, m, total):
        c = m * TURN
        if rnd > 0:
            wait_both(column, rnd, 0, m)

        def part(h, carry):
            first_part(rnd, c + h)
            return carry

        lax.fori_loop(0, TURN, part, 0)
        if send:
            start_both(plane, rnd, 1, c)
        if MERGE[rnd][0] == TURN:
            wait_both(plane, rnd, 0, c)
        total = lax.fori_loop(0, TURN, lambda h, t: first_rest(rnd, c + h, t), total)
        start_both(column, rnd, 1, m)
        return total

    def fold(x):
        while x.shape[0] > GROUP:
            half = x.shape[0] // 2
            x = x[:half] + x[half:]
        return x

    def second_part(rnd, c, total):
        cols = outer_columns(rnd, 1, c)
        field, kv = fields[rnd], kvs[rnd]

        def rest(b, carry):
            acc, totals = carry
            row = pl.multiple_of(c * CHUNK + b * BLOCK, BLOCK)
            rows = pl.ds(row, BLOCK)
            wide = pl.ds(PAD + row, BLOCK)
            out = own_part(kv, cols, row, b)
            out[0] = out[0] - (precv[rnd, 0, rows] - field[0, wide])
            out[last] = out[last] - (precv[rnd, 1, rows] - field[last, wide])
            for d in range(days):
                image = SCALE * out[d]
                if rnd == 0:
                    base = sres[d, rows]
                    residual = 0.0 - (image + base)
                    value = residual * inv[d, rows]
                    r0[d, rows] = residual
                    p0p[d, wide] = value
                else:
                    image = image + weight[d, rows] * field[d, wide]
                    if rnd == 1:
                        value = image * inv[d, rows]
                        q0[d, rows] = image
                        up[d, wide] = value
                        p = field[d, wide]
                        y, z = r0[d, rows] - image, p - value
                        totals = (
                            totals[0] + fold(y * p),
                            totals[1] + fold(y * z),
                            totals[2] + fold(y * value),
                            totals[3] + fold(image * value),
                        )
                    else:
                        sres[d, rows] = image
                if rnd < ROUNDS - 1:
                    acc = acc + gather(value, d, b)
            return acc, totals

        acc, total = unrolled(blocks, rest, (zeros, total))
        if rnd < ROUNDS - 1:
            if MERGE[rnd + 1][0] == 1:
                start_both(plane, rnd + 1, 0, c)
            csend[rnd + 1, 0, c] = acc
        return total

    def second_k(rnd, m, total):
        c = m * TURN
        wait_both(column, rnd, 1, m)
        wait_both(plane, rnd, 1, c)
        total = lax.fori_loop(0, TURN, lambda h, t: second_part(rnd, c + h, t), total)
        if rnd < ROUNDS - 1 and MERGE[rnd + 1][0] == TURN:
            start_both(plane, rnd + 1, 0, c)
        if rnd < ROUNDS - 1:
            start_both(column, rnd + 1, 0, m)
        return total

    def peer_copy(stage, k):
        peers = (day_peer, lon_peer)[stage]
        return pltpu.make_async_remote_copy(
            src_ref=redsend.at[stage], dst_ref=redrecv.at[stage, k],
            send_sem=red_ss.at[stage], recv_sem=red_rs.at[stage],
            device_id=peers[k], device_id_type=MESH,
        )

    def all_peers(stage):
        others = redrecv.at[stage, pl.ds(1, (n_day, n_lon)[stage] - 1)]
        return pltpu.make_async_remote_copy(
            src_ref=others, dst_ref=others, send_sem=red_ss.at[stage], recv_sem=red_rs.at[stage],
            device_id=(day_peer, lon_peer)[stage][1], device_id_type=MESH,
        )

    def reduce_start(stage, rows):
        redsend[stage] = rows
        for k in range(1, (n_day, n_lon)[stage]):
            peer_copy(stage, k).start()

    def reduce_wait(stage):
        n = (n_day, n_lon)[stage]
        total = redsend[stage]
        all_peers(stage).wait_recv()
        for k in range(1, n):
            total = total + redrecv[stage, k]
        return total

    def as_rows(values):
        row = lax.broadcasted_iota(jnp.int32, (GROUP, lons), 0)
        out = zeros
        for i, v in enumerate(values):
            out = jnp.where(row == i, jnp.sum(v, axis=0, keepdims=True), out)
        return out

    loads[0].wait()
    for ref in (latp, p0p, up, kv0, kv1, kv2):
        for d in range(days):
            ref[d, pl.ds(0, PAD)] = zeros
            ref[d, pl.ds(PAD + lats, PAD)] = zeros

    def first_columns(c, carry):
        def step(b, acc):
            row = pl.multiple_of(c * CHUNK + b * BLOCK, BLOCK)
            for d in range(days):
                acc = acc + gather(latp[d, pl.ds(PAD + row, BLOCK)], d, b)
            return acc

        csend[0, 0, c] = unrolled(blocks, step, zeros)
        return carry

    lax.fori_loop(0, chunks, first_columns, 0)
    start_both(column, 0, 0, 0)

    for copy in loads[1:]:
        copy.wait()

    def prepare(b, carry):
        row = pl.multiple_of(b * SMALL, SMALL)
        rows = pl.ds(row, SMALL)
        at = row + lax.broadcasted_iota(jnp.int32, (SMALL, lons), 0)
        near = 6.0 - jnp.where(at == 0, 1.0, 0.0) - jnp.where(at == lats - 1, 1.0, 0.0)
        for d in range(days):
            mask = land[d, rows].astype(jnp.float32)
            w = mask * jnp.exp(latp[d, pl.ds(PAD + row, SMALL)])
            diag = rs6[d, rows] + 6.0
            rs6[d, rows] = diag
            weight[d, rows] = w
            inv[d, rows] = 1.0 / (SCALE * (diag * diag + near) + w)
            sres[d, rows] = w - mask * cnt[d, rows].astype(jnp.float32)
        return carry

    lax.fori_loop(0, lats // SMALL, prepare, 0)

    turns = chunks // TURN
    sums = []
    wait_both(column, 0, 0, 0)
    for rnd in range(ROUNDS - 1):
        sums += lax.fori_loop(0, turns, functools.partial(first_k, rnd, True), ((), (zeros,))[rnd])
        sums += lax.fori_loop(0, turns, functools.partial(second_k, rnd), ((), (zeros,) * 4)[rnd])

    rnd = ROUNDS - 1
    total = lax.fori_loop(0, turns - HELD, functools.partial(first_k, rnd, True), (zeros,) * 3)
    sums += lax.fori_loop(turns - HELD, turns, functools.partial(first_k, rnd, False), total)
    reduce_start(0, as_rows(sums))
    for c in range(turns - HELD, turns):
        start_both(plane, rnd, 1, c * TURN)
    lax.fori_loop(0, turns - HELD, functools.partial(second_k, rnd), ())
    reduce_start(1, reduce_wait(0))
    lax.fori_loop(turns - HELD, turns, functools.partial(second_k, rnd), ())

    for kind in range(2):
        pltpu.make_async_remote_copy(
            src_ref=psend, dst_ref=precv, send_sem=plane_ss.at[kind], recv_sem=plane_rs.at[kind, 0, 0],
            device_id=sides[0], device_id_type=MESH,
        ).wait_send()
    for side in range(2):
        pltpu.make_async_remote_copy(
            src_ref=csend, dst_ref=crecv.at[1 - side], send_sem=col_ss.at[side], recv_sem=col_rs.at[0, 0, 0],
            device_id=beside[side], device_id_type=MESH,
        ).wait_send()
    all_peers(0).wait_send()

    all_sums = jnp.sum(reduce_wait(1), axis=1, keepdims=True)
    m1, n1, n2, n3, m2, zz, zu, uu = [jnp.broadcast_to(all_sums[i:i + 1], (1, lons)) for i in range(GROUP)]
    extra = n1 / m1
    a0 = 1.0 + extra
    rz1 = n2 - 2.0 * extra * n3 + extra * extra * m2
    beta = rz1 / (m1 + n1)
    zq = n3 - extra * m2
    zhz = zz - 2.0 * extra * zu + extra * extra * uu
    a1 = rz1 / (zhz + 2.0 * beta * zq + beta * beta * m1)
    coefs[0:1] = a0 + a1 * (1.0 + beta)
    coefs[1:2] = a0 * a1

    all_peers(1).wait_send()


def solution(mesh):
    names = tuple(mesh.axis_names)
    n_day, n_lon = mesh.shape["day"], mesh.shape["lon"]
    spec = P("day", None, "lon")

    def per_device(latent, range_sq, counts, land):
        days, lats, lons = latent.shape
        chunks = lats // CHUNK
        f32 = jnp.float32
        whole = (days, lats, lons)
        padded = (days, lats + 2 * PAD, lons)
        vmem = pltpu.VMEM
        dma = pltpu.SemaphoreType.DMA
        p0, u, r0, q0, s, coefs = pl.pallas_call(
            functools.partial(kernel, names, n_day, n_lon),
            out_shape=[
                vmem(padded, f32), vmem(padded, f32), vmem(whole, f32), vmem(whole, f32), vmem(whole, f32),
                vmem((2, lons), f32),
            ],
            in_specs=[pl.BlockSpec(memory_space=pl.ANY)] * 4,
            out_specs=[pl.BlockSpec(memory_space=pltpu.VMEM)] * 6,
            scratch_shapes=[
                vmem(padded, f32), vmem(whole, f32), vmem(whole, jnp.int32), vmem(whole, jnp.int32),
                vmem(whole, f32), vmem(whole, f32),
                vmem(padded, f32), vmem(padded, f32), vmem(padded, f32),
                vmem((ROUNDS, 2, lats, lons), f32), vmem((ROUNDS, 2, lats, lons), f32),
                vmem((ROUNDS, 2, lats, lons), f32),
                vmem((ROUNDS, 2, chunks, GROUP, lons), f32), vmem((2, ROUNDS, 2, chunks, GROUP, lons), f32),
                vmem((2, GROUP, lons), f32), vmem((2, n_lon, GROUP, lons), f32),
                dma((2,)), dma((2, chunks + chunks // TURN, 2)),
                dma((2,)), dma((2, 2 * chunks // TURN, 2)),
                dma((2,)), dma((2,)), dma((4,)),
            ],
            compiler_params=pltpu.CompilerParams(
                collective_id=0, has_side_effects=True, vmem_limit_bytes=44 << 20
            ),
        )(latent, range_sq, counts, land)
        body = slice(PAD, PAD + lats)
        step = coefs[0] * p0[:, body] - coefs[1] * u[:, body]
        residual = r0 - coefs[0] * q0 + coefs[1] * s
        return step, residual

    return jax.shard_map(per_device, mesh=mesh, in_specs=(spec,) * 4, out_specs=(spec, spec), check_vma=False)
```

```python
import functools

import jax
import jax.numpy as jnp
from jax import lax
from jax.experimental import pallas as pl
from jax.experimental.pallas import tpu as pltpu
from jax.sharding import PartitionSpec as P

ROUNDS = 3
SCALE = 0.02
PAD = 8
GROUP = 8
CHUNK = 128
MERGE = ((2, 2), (2, 2), (1, 2))
TURN = 2
BLOCK = 128
SMALL = 64
HELD = 2
MESH = pl.DeviceIdType.MESH


def kernel(
    names, n_day, n_lon,
    lat_h, rs_h, cnt_h, land_h, p0p, up, r0, q0, sres, coefs,
    latp, rs6, cnt, land, weight, inv, kv0, kv1, kv2,
    psend, vrecv, precv, csend, crecv, redsend, redrecv,
    plane_ss, plane_rs, col_ss, col_rs, red_ss, red_rs, in_sem,
):
    days, lats, lons = rs6.shape
    last = days - 1
    chunks = lats // CHUNK
    groups = CHUNK // GROUP
    blocks = CHUNK // BLOCK
    per_block = BLOCK // GROUP
    me_d = lax.axis_index("day")
    me_l = lax.axis_index("lon")

    def device(day, lon):
        where = {"day": day, "lon": lon}
        return tuple(where[n] for n in names)

    day_peer = [device(lax.rem(me_d + k, n_day), me_l) for k in range(n_day)]
    lon_peer = [device(me_d, lax.rem(me_l + k, n_lon)) for k in range(n_lon)]
    sides = (day_peer[n_day - 1], day_peer[1])
    beside = (lon_peer[n_lon - 1], lon_peer[1])

    body = pl.ds(PAD, lats)
    loads = [
        pltpu.make_async_copy(lat_h, latp.at[:, body], in_sem.at[0]),
        pltpu.make_async_copy(rs_h, rs6, in_sem.at[1]),
        pltpu.make_async_copy(land_h, land, in_sem.at[2]),
        pltpu.make_async_copy(cnt_h, cnt, in_sem.at[3]),
    ]
    loads[0].start()
    barrier = pltpu.get_barrier_semaphore()
    for peer in day_peer[1:] + lon_peer[1:]:
        pl.semaphore_signal(barrier, inc=1, device_id=peer, device_id_type=MESH)
    pl.semaphore_wait(barrier, n_day + n_lon - 2)

    fields = (latp, p0p, up)
    kvs = (kv0, kv1, kv2)
    edges = (0, last)

    def slot(rnd, c, merge):
        at = c // merge if isinstance(c, int) else lax.div(c, merge)
        return at + (chunks if rnd == 1 else 0)

    def plane(rnd, kind, c, side):
        size = CHUNK * MERGE[rnd][kind]
        rows = pl.ds(c * CHUNK, size)
        if kind == 0:
            if rnd == 0:
                src = lat_h.at[edges[side], rows]
            else:
                src = fields[rnd].at[edges[side], pl.ds(PAD + c * CHUNK, size)]
            dst = vrecv.at[rnd, 1 - side, rows]
        else:
            src = psend.at[rnd, side, rows]
            dst = precv.at[rnd, 1 - side, rows]
        return pltpu.make_async_remote_copy(
            src_ref=src, dst_ref=dst,
            send_sem=plane_ss.at[kind], recv_sem=plane_rs.at[kind, slot(rnd, c, MERGE[rnd][kind]), 1 - side],
            device_id=sides[side], device_id_type=MESH,
        )

    def column(rnd, kind, m, side):
        tiles = pl.ds(0, chunks) if rnd == kind == 0 else pl.ds(m * TURN, TURN)
        return pltpu.make_async_remote_copy(
            src_ref=csend.at[rnd, kind, tiles], dst_ref=crecv.at[1 - side, rnd, kind, tiles],
            send_sem=col_ss.at[side], recv_sem=col_rs.at[kind, m + (chunks // TURN if rnd == 1 else 0), 1 - side],
            device_id=beside[side], device_id_type=MESH,
        )

    def unrolled(n, body, carry):
        for i in range(n):
            carry = body(i, carry)
        return carry

    def start_both(copy, rnd, kind, c):
        copy(rnd, kind, c, 0).start()
        copy(rnd, kind, c, 1).start()

    def wait_both(copy, rnd, kind, c):
        copy(rnd, kind, c, 0).wait_recv()
        copy(rnd, kind, c, 1).wait_recv()

    for c in range(0, chunks, MERGE[0][0]):
        start_both(plane, 0, 0, c)
    for copy in loads[1:]:
        copy.start()

    lane = lax.broadcasted_iota(jnp.int32, (GROUP, lons), 1)
    pair = ((lane + 1) & (lons - 1)) >> 1
    lane_block = lax.broadcasted_iota(jnp.int32, (BLOCK, lons), 1)
    at_low = lane_block == 0
    at_high = lane_block == lons - 1
    even = (lane & 1) == 0
    zeros = jnp.zeros((GROUP, lons), jnp.float32)

    def gather(tile, d, b):
        acc = zeros
        for k in range(per_block):
            j = d * groups + b * per_block + k
            acc = jnp.where(pair == j, pltpu.roll(tile[k * GROUP:(k + 1) * GROUP], (2 * j) % lons, 1), acc)
        return acc

    def outer_columns(rnd, kind, c):
        low = crecv[0, rnd, kind, c]
        high = crecv[1, rnd, kind, c]
        return jnp.where(even, pltpu.roll(low, 1, 1), pltpu.roll(high, lons - 1, 1))

    def along_lon(x, cols, d, b):
        outer = jnp.concatenate(
            [pltpu.roll(cols, (0 - 2 * (d * groups + b * per_block + k)) % lons, 1) for k in range(per_block)], axis=0
        )
        return jnp.where(at_low, outer, pltpu.roll(x, 1, 1)) + jnp.where(at_high, outer, pltpu.roll(x, lons - 1, 1))

    def own_part(ref, cols, row, b):
        x = [ref[d, pl.ds(PAD + row, BLOCK)] for d in range(days)]
        out = []
        for d in range(days):
            near = ref[d, pl.ds(PAD - 1 + row, BLOCK)] + ref[d, pl.ds(PAD + 1 + row, BLOCK)]
            near = near + along_lon(x[d], cols, d, b)
            if d > 0:
                near = near + x[d - 1]
            if d < last:
                near = near + x[d + 1]
            out.append(rs6[d, pl.ds(row, BLOCK)] * x[d] - near)
        return out

    def first_part(rnd, c):
        cols = outer_columns(rnd, 0, c)
        field, kv = fields[rnd], kvs[rnd]

        def partial(b, carry):
            row = pl.multiple_of(c * CHUNK + b * BLOCK, BLOCK)
            out = own_part(field, cols, row, b)
            rows = pl.ds(row, BLOCK)
            psend[rnd, 0, rows] = out[0]
            psend[rnd, 1, rows] = out[last]
            for d in range(1, last):
                kv[d, pl.ds(PAD + row, BLOCK)] = out[d]
            return carry

        unrolled(blocks, partial, 0)

    def first_rest(rnd, c, total):
        if MERGE[rnd][0] == 1:
            wait_both(plane, rnd, 0, c)
        field, kv = fields[rnd], kvs[rnd]

        def complete(b, carry):
            acc, totals = carry
            row = pl.multiple_of(c * CHUNK + b * BLOCK, BLOCK)
            rows = pl.ds(row, BLOCK)
            wide = pl.ds(PAD + row, BLOCK)
            for d in range(days):
                if d == 0 or d == last:
                    side = 0 if d == 0 else 1
                    tile = psend[rnd, side, rows] - vrecv[rnd, side, rows]
                    kv[d, wide] = tile
                else:
                    tile = kv[d, wide]
                acc = acc + gather(tile, d, b)
                if rnd == 1:
                    p = field[d, wide]
                    totals = (totals[0] + fold(SCALE * tile * tile + weight[d, rows] * p * p),)
                if rnd == 2:
                    w, u = weight[d, rows], field[d, wide]
                    z = p0p[d, wide] - u
                    kz = kv1[d, wide] - tile
                    skz, wz = SCALE * kz, w * z
                    totals = (
                        totals[0] + fold(skz * kz + wz * z),
                        totals[1] + fold(skz * tile + wz * u),
                        totals[2] + fold(SCALE * tile * tile + w * u * u),
                    )
            return acc, totals

        acc, total = unrolled(blocks, complete, (zeros, total))
        csend[rnd, 1, c] = acc
        return total

    def first_k(rnd, send, m, total):
        c = m * TURN
        if rnd > 0:
            wait_both(column, rnd, 0, m)

        def part(h, carry):
            first_part(rnd, c + h)
            return carry

        lax.fori_loop(0, TURN, part, 0)
        if send:
            start_both(plane, rnd, 1, c)
        if MERGE[rnd][0] == TURN:
            wait_both(plane, rnd, 0, c)
        total = lax.fori_loop(0, TURN, lambda h, t: first_rest(rnd, c + h, t), total)
        start_both(column, rnd, 1, m)
        return total

    def fold(x):
        while x.shape[0] > GROUP:
            half = x.shape[0] // 2
            x = x[:half] + x[half:]
        return x

    def second_part(rnd, c, total):
        cols = outer_columns(rnd, 1, c)
        field, kv = fields[rnd], kvs[rnd]

        def rest(b, carry):
            acc, totals = carry
            row = pl.multiple_of(c * CHUNK + b * BLOCK, BLOCK)
            rows = pl.ds(row, BLOCK)
            wide = pl.ds(PAD + row, BLOCK)
            out = own_part(kv, cols, row, b)
            out[0] = out[0] - (precv[rnd, 0, rows] - field[0, wide])
            out[last] = out[last] - (precv[rnd, 1, rows] - field[last, wide])
            for d in range(days):
                image = SCALE * out[d]
                if rnd == 0:
                    base = sres[d, rows]
                    residual = 0.0 - (image + base)
                    value = residual * inv[d, rows]
                    r0[d, rows] = residual
                    p0p[d, wide] = value
                else:
                    image = image + weight[d, rows] * field[d, wide]
                    if rnd == 1:
                        value = image * inv[d, rows]
                        q0[d, rows] = image
                        up[d, wide] = value
                        p = field[d, wide]
                        y, z = r0[d, rows] - image, p - value
                        totals = (
                            totals[0] + fold(y * p),
                            totals[1] + fold(y * z),
                            totals[2] + fold(y * value),
                            totals[3] + fold(image * value),
                        )
                    else:
                        sres[d, rows] = image
                if rnd < ROUNDS - 1:
                    acc = acc + gather(value, d, b)
            return acc, totals

        acc, total = unrolled(blocks, rest, (zeros, total))
        if rnd < ROUNDS - 1:
            if MERGE[rnd + 1][0] == 1:
                start_both(plane, rnd + 1, 0, c)
            csend[rnd + 1, 0, c] = acc
        return total

    def second_k(rnd, m, total):
        c = m * TURN
        wait_both(column, rnd, 1, m)
        wait_both(plane, rnd, 1, c)
        total = lax.fori_loop(0, TURN, lambda h, t: second_part(rnd, c + h, t), total)
        if rnd < ROUNDS - 1 and MERGE[rnd + 1][0] == TURN:
            start_both(plane, rnd + 1, 0, c)
        if rnd < ROUNDS - 1:
            start_both(column, rnd + 1, 0, m)
        return total

    def peer_copy(stage, k):
        peers = (day_peer, lon_peer)[stage]
        return pltpu.make_async_remote_copy(
            src_ref=redsend.at[stage], dst_ref=redrecv.at[stage, k],
            send_sem=red_ss.at[stage], recv_sem=red_rs.at[stage],
            device_id=peers[k], device_id_type=MESH,
        )

    def all_peers(stage):
        others = redrecv.at[stage, pl.ds(1, (n_day, n_lon)[stage] - 1)]
        return pltpu.make_async_remote_copy(
            src_ref=others, dst_ref=others, send_sem=red_ss.at[stage], recv_sem=red_rs.at[stage],
            device_id=(day_peer, lon_peer)[stage][1], device_id_type=MESH,
        )

    def reduce_start(stage, rows):
        redsend[stage] = rows
        for k in range(1, (n_day, n_lon)[stage]):
            peer_copy(stage, k).start()

    def reduce_wait(stage):
        n = (n_day, n_lon)[stage]
        total = redsend[stage]
        all_peers(stage).wait_recv()
        for k in range(1, n):
            total = total + redrecv[stage, k]
        return total

    def as_rows(values):
        row = lax.broadcasted_iota(jnp.int32, (GROUP, lons), 0)
        out = zeros
        for i, v in enumerate(values):
            out = jnp.where(row == i, jnp.sum(v, axis=0, keepdims=True), out)
        return out

    loads[0].wait()
    for ref in (latp, p0p, up, kv0, kv1, kv2):
        for d in range(days):
            ref[d, pl.ds(0, PAD)] = zeros
            ref[d, pl.ds(PAD + lats, PAD)] = zeros

    def first_columns(c, carry):
        def step(b, acc):
            row = pl.multiple_of(c * CHUNK + b * BLOCK, BLOCK)
            for d in range(days):
                acc = acc + gather(latp[d, pl.ds(PAD + row, BLOCK)], d, b)
            return acc

        csend[0, 0, c] = unrolled(blocks, step, zeros)
        return carry

    lax.fori_loop(0, chunks, first_columns, 0)
    start_both(column, 0, 0, 0)

    for copy in loads[1:]:
        copy.wait()

    def prepare(b, carry):
        row = pl.multiple_of(b * SMALL, SMALL)
        rows = pl.ds(row, SMALL)
        at = row + lax.broadcasted_iota(jnp.int32, (SMALL, lons), 0)
        near = 6.0 - jnp.where(at == 0, 1.0, 0.0) - jnp.where(at == lats - 1, 1.0, 0.0)
        for d in range(days):
            mask = land[d, rows].astype(jnp.float32)
            w = mask * jnp.exp(latp[d, pl.ds(PAD + row, SMALL)])
            diag = rs6[d, rows] + 6.0
            rs6[d, rows] = diag
            weight[d, rows] = w
            inv[d, rows] = 1.0 / (SCALE * (diag * diag + near) + w)
            sres[d, rows] = w - mask * cnt[d, rows].astype(jnp.float32)
        return carry

    lax.fori_loop(0, lats // SMALL, prepare, 0)

    turns = chunks // TURN
    sums = []
    wait_both(column, 0, 0, 0)
    for rnd in range(ROUNDS - 1):
        sums += lax.fori_loop(0, turns, functools.partial(first_k, rnd, True), ((), (zeros,))[rnd])
        sums += lax.fori_loop(0, turns, functools.partial(second_k, rnd), ((), (zeros,) * 4)[rnd])

    rnd = ROUNDS - 1
    total = lax.fori_loop(0, turns - HELD, functools.partial(first_k, rnd, True), (zeros,) * 3)
    sums += lax.fori_loop(turns - HELD, turns, functools.partial(first_k, rnd, False), total)
    reduce_start(0, as_rows(sums))
    for c in range(turns - HELD, turns):
        start_both(plane, rnd, 1, c * TURN)
    lax.fori_loop(0, turns - HELD, functools.partial(second_k, rnd), ())
    reduce_start(1, reduce_wait(0))
    lax.fori_loop(turns - HELD, turns, functools.partial(second_k, rnd), ())

    for kind in range(2):
        pltpu.make_async_remote_copy(
            src_ref=psend, dst_ref=precv, send_sem=plane_ss.at[kind], recv_sem=plane_rs.at[kind, 0, 0],
            device_id=sides[0], device_id_type=MESH,
        ).wait_send()
    for side in range(2):
        pltpu.make_async_remote_copy(
            src_ref=csend, dst_ref=crecv.at[1 - side], send_sem=col_ss.at[side], recv_sem=col_rs.at[0, 0, 0],
            device_id=beside[side], device_id_type=MESH,
        ).wait_send()
    all_peers(0).wait_send()

    all_sums = jnp.sum(reduce_wait(1), axis=1, keepdims=True)
    m1, n1, n2, n3, m2, zz, zu, uu = [jnp.broadcast_to(all_sums[i:i + 1], (1, lons)) for i in range(GROUP)]
    extra = n1 / m1
    a0 = 1.0 + extra
    rz1 = n2 - 2.0 * extra * n3 + extra * extra * m2
    beta = rz1 / (m1 + n1)
    zq = n3 - extra * m2
    zhz = zz - 2.0 * extra * zu + extra * extra * uu
    a1 = rz1 / (zhz + 2.0 * beta * zq + beta * beta * m1)
    coefs[0:1] = a0 + a1 * (1.0 + beta)
    coefs[1:2] = a0 * a1

    all_peers(1).wait_send()


def finish(p0p, up, r0, q0, s, coefs, step_h, res_h, step, res, sems):
    days, lats, lons = r0.shape
    chunks = lats // CHUNK
    coef_p = jnp.broadcast_to(coefs[0:1], (SMALL, lons))
    coef_u = jnp.broadcast_to(coefs[1:2], (SMALL, lons))

    def copies(c):
        rows = pl.ds(c * CHUNK, CHUNK)
        return (
            pltpu.make_async_copy(step.at[:, rows], step_h.at[:, rows], sems.at[0, c]),
            pltpu.make_async_copy(res.at[:, rows], res_h.at[:, rows], sems.at[1, c]),
        )

    def one(c, carry):
        for b in range(CHUNK // SMALL):
            row = pl.multiple_of(c * CHUNK + b * SMALL, SMALL)
            rows, wide = pl.ds(row, SMALL), pl.ds(PAD + row, SMALL)
            for d in range(days):
                step[d, rows] = coef_p * p0p[d, wide] - coef_u * up[d, wide]
                res[d, rows] = r0[d, rows] - coef_p * q0[d, rows] + coef_u * s[d, rows]
        for copy in copies(c):
            copy.start()
        return carry

    lax.fori_loop(0, chunks, one, 0)
    for c in range(chunks):
        for copy in copies(c):
            copy.wait()


def solution(mesh):
    names = tuple(mesh.axis_names)
    n_day, n_lon = mesh.shape["day"], mesh.shape["lon"]
    spec = P("day", None, "lon")

    def per_device(latent, range_sq, counts, land):
        days, lats, lons = latent.shape
        chunks = lats // CHUNK
        f32 = jnp.float32
        whole = (days, lats, lons)
        padded = (days, lats + 2 * PAD, lons)
        vmem = pltpu.VMEM
        dma = pltpu.SemaphoreType.DMA
        p0, u, r0, q0, s, coefs = pl.pallas_call(
            functools.partial(kernel, names, n_day, n_lon),
            out_shape=[
                vmem(padded, f32), vmem(padded, f32), vmem(whole, f32), vmem(whole, f32), vmem(whole, f32),
                vmem((2, lons), f32),
            ],
            in_specs=[pl.BlockSpec(memory_space=pl.ANY)] * 4,
            out_specs=[pl.BlockSpec(memory_space=pltpu.VMEM)] * 6,
            scratch_shapes=[
                vmem(padded, f32), vmem(whole, f32), vmem(whole, jnp.int32), vmem(whole, jnp.int32),
                vmem(whole, f32), vmem(whole, f32),
                vmem(padded, f32), vmem(padded, f32), vmem(padded, f32),
                vmem((ROUNDS, 2, lats, lons), f32), vmem((ROUNDS, 2, lats, lons), f32),
                vmem((ROUNDS, 2, lats, lons), f32),
                vmem((ROUNDS, 2, chunks, GROUP, lons), f32), vmem((2, ROUNDS, 2, chunks, GROUP, lons), f32),
                vmem((2, GROUP, lons), f32), vmem((2, n_lon, GROUP, lons), f32),
                dma((2,)), dma((2, chunks + chunks // TURN, 2)),
                dma((2,)), dma((2, 2 * chunks // TURN, 2)),
                dma((2,)), dma((2,)), dma((4,)),
            ],
            compiler_params=pltpu.CompilerParams(
                collective_id=0, has_side_effects=True, vmem_limit_bytes=44 << 20
            ),
        )(latent, range_sq, counts, land)
        held = [pltpu.with_memory_space_constraint(v, pltpu.VMEM) for v in (p0, u, r0, q0, s, coefs)]
        step, residual = pl.pallas_call(
            finish,
            out_shape=[jax.ShapeDtypeStruct(whole, f32)] * 2,
            in_specs=[pl.BlockSpec(memory_space=pltpu.VMEM)] * 6,
            out_specs=[pl.BlockSpec(memory_space=pl.ANY)] * 2,
            scratch_shapes=[vmem(whole, f32), vmem(whole, f32), dma((2, chunks))],
            compiler_params=pltpu.CompilerParams(vmem_limit_bytes=16 << 20),
        )(*held)
        return step, residual

    return jax.shard_map(per_device, mesh=mesh, in_specs=(spec,) * 4, out_specs=(spec, spec), check_vma=False)
```
